512 devices in a mesh: group: 16 (over y, core), peer: 32 (over x, z).
Axes of the slice: x: 4, y: 8, z: 8, core: 2. Of those that a mesh axis runs over, the one named last changes fastest.
Arguments:
- trace_rows: bfloat16 [1024, 8, 32, 512], P(('group', 'peer')), may hold values from -40 to 40
- upstream: bfloat16 [1024, 8, 32, 512], P(('group', 'peer')), may hold values from -6 to 6
- counts: int32 [16, 64], P('group', 'peer'), may hold values from 1 to 8, 256 in all within a row
- w_query: bfloat16 [512, 512], P('peer'), may hold values from -0.25 to 0.25
- w_key: bfloat16 [512, 512], P('peer'), may hold values from -0.25 to 0.25
- w_value: bfloat16 [512, 512], P('peer'), may hold values from -0.25 to 0.25
- w_out: bfloat16 [512, 512], P('peer'), may hold values from -0.25 to 0.25
Outputs:
- trace_grads: bfloat16 [1024, 8, 32, 512], P(('group', 'peer'))
- query_grad: float32 [512, 512], P('peer')
- key_grad: float32 [512, 512], P('peer')
- value_grad: float32 [512, 512], P('peer')
- output_grad: float32 [512, 512], P('peer')
The draws below stay inside these ranges and needn't reach their ends.
Inputs may be any that keep to these rules, and one draw needn't show every extreme that they name: In each row of counts (one group) the 64 counts sum to exactly 256, and the largest is 8.
All inputs are finite; a program needn't handle non-finite values.
Results may differ from the reference program's by a relative error of at most 0.03.
Values may be sent and summed in bfloat16 or wider, within the bound.
No kernel may reach another device: no remote copies, remote signals or barrier semaphores. Data moves between devices by JAX's collectives and lax.ppermute only.
A program may use at most 64 MiB of HBM per device.

```python
import math
import jax
import jax.numpy as jnp
import numpy as np
from jax import lax

D = 512
HEADS = 8
HEAD = 64
INNER = 512
TRACE_LEN = 32
MOST = 8
SLOTS = 16
VIEWS_GROUP = 64
VIEWS = 1024
GROUP_ROWS = 256
LIVE_TOKENS = 131072
N_GROUP = 16
N_PEER = 32


def draw_trace_rows(key, part):
    key = jax.random.fold_in(key, 7)
    row_key, column_key, base_key = jax.random.split(key, 3)
    full_shape = (VIEWS, MOST, TRACE_LEN, D)
    row_scale = jnp.exp(jax.random.uniform(row_key, (VIEWS, MOST, TRACE_LEN, 1), jnp.float32, math.log(0.5), math.log(5.0)))
    column_scale = jnp.exp(jax.random.uniform(column_key, (1, 1, 1, D), jnp.float32, math.log(0.5), math.log(2.0)))
    base_values = jnp.clip(jax.random.normal(base_key, full_shape, jnp.float32), -4.0, 4.0)
    return (base_values * row_scale * column_scale).astype(jnp.bfloat16)


def shard_levels(own_key, shape, cuts, least, largest):
    def one(dim, parts):
        draws = jax.random.uniform(jax.random.fold_in(jax.random.fold_in(own_key, 6), dim), (parts,), jnp.float32, least / len(cuts), largest / len(cuts))
        return jnp.repeat(jnp.exp(draws), shape[dim] // parts).reshape((-1,) + (1,) * (len(shape) - dim - 1))

    gain = one(*cuts[0])
    for cut in cuts[1:]:
        gain = gain * one(*cut)
    return gain


def profile(count, total, limit, slope):
    loads = [(1 << 20) // math.isqrt(rank ** slope) + 1 for rank in range(2, count + 1)]
    rest, given = total - limit - (count - 1), [1] * (count - 1)
    while rest > 0:
        free = [i for i in range(count - 1) if given[i] < limit]
        pool, left = sum([loads[i] for i in free]), rest
        for i in free:
            addition = min(limit - given[i], max(1, left * loads[i] // pool), rest)
            given[i] = given[i] + addition
            rest = rest - addition
    return np.array([limit] + given)


def ragged_sizes(own_key, amount, total, reach, skew):
    if amount == 2:
        one = jax.random.randint(own_key, (), max(1, total - reach), min(reach, total - 1) + 1)
        return jnp.stack([one, total - one])
    sizes = jnp.asarray(profile(amount, total, reach, skew), jnp.int32)
    twos = (amount - 1) // 2
    donor, sink = sizes[1:1 + 2 * twos:2], sizes[2:2 + 2 * twos:2]
    room = jnp.minimum(donor - 1, reach - sink)
    passed = jax.random.randint(jax.random.fold_in(own_key, 1), (twos,), 0, 1 << 20) % (room + 1)
    sizes = sizes.at[1:1 + 2 * twos:2].set(donor - passed).at[2:2 + 2 * twos:2].set(sink + passed)
    return sizes[jax.random.permutation(jax.random.fold_in(own_key, 2), amount)]


def bell_draw(rng, extent, spread, limit, cuts=(), kind=jnp.bfloat16):
    drawn = spread * jax.random.normal(rng, extent, jnp.float32)
    if cuts:
        drawn = drawn * shard_levels(rng, extent, cuts, -0.22, 0.18)
    return jnp.clip(drawn, -limit, limit).astype(kind)


def setup_inputs(seed: int = 0) -> dict:
    arg_keys = jax.random.split(jax.random.key(seed), 8)
    return {
        "trace_rows": draw_trace_rows(jax.random.fold_in(arg_keys[7], 71), 0),
        "upstream": bell_draw(arg_keys[1], (VIEWS, MOST, TRACE_LEN, D), 1.0, 6.0, ((0, 512),)),
        "counts": jax.vmap(lambda own: ragged_sizes(own, VIEWS_GROUP, GROUP_ROWS, MOST, 2))(jax.random.split(arg_keys[2], N_GROUP)).reshape((N_GROUP, VIEWS_GROUP)).astype(jnp.int32),
        "w_query": bell_draw(arg_keys[3], (D, INNER), D ** -0.5, 0.25, ((0, 32),)),
        "w_key": bell_draw(arg_keys[4], (D, INNER), D ** -0.5, 0.25, ((0, 32),)),
        "w_value": bell_draw(arg_keys[5], (D, INNER), D ** -0.5, 0.25, ((0, 32),)),
        "w_out": bell_draw(arg_keys[6], (INNER, D), INNER ** -0.5, 0.25, ((0, 32),)),
    }


score_gain = 6.0
tiny_eps = 1e-06

def unit_heads(values):
    split_heads = values.reshape(values.shape[0], values.shape[1], HEADS, HEAD)
    inv_scale = lax.rsqrt(lax.optimization_barrier(jnp.mean(split_heads * split_heads, axis=-1, keepdims=True)) + tiny_eps)
    return (split_heads * inv_scale, inv_scale)

def rounded(values):
    return lax.optimization_barrier(values.astype(jnp.bfloat16)).astype(jnp.float32)

def row_backward(rows, grad_in, w_query, w_key, w_value, w_out):
    row_count = rows.shape[0]
    token_count = row_count * TRACE_LEN
    flat_rows = rows.reshape(token_count, D).astype(jnp.float32)
    inv_rms = lax.rsqrt(lax.optimization_barrier(jnp.mean(flat_rows * flat_rows, axis=-1, keepdims=True)) + tiny_eps)
    scaled = flat_rows * inv_rms
    normed = scaled.astype(jnp.bfloat16)
    queries = jnp.dot(normed, w_query, preferred_element_type=jnp.float32).reshape(row_count, TRACE_LEN, INNER)
    keys_full = jnp.dot(normed, w_key, preferred_element_type=jnp.float32).reshape(row_count, TRACE_LEN, INNER)
    values_full = jnp.dot(normed, w_value, preferred_element_type=jnp.float32)
    q_unit, q_scale = unit_heads(queries)
    k_unit, k_scale = unit_heads(keys_full)
    q_half = rounded(q_unit)
    k_half = rounded(k_unit)
    v_half = rounded(values_full).reshape(row_count, TRACE_LEN, HEADS, HEAD)
    scores = jnp.einsum('rqhd,rkhd->rhqk', q_half, k_half) * (score_gain / HEAD)
    exp_scores = jnp.exp(scores)
    att_probs = exp_scores / lax.optimization_barrier(jnp.sum(exp_scores, axis=-1, keepdims=True))
    probs_half = rounded(att_probs)
    attended = jnp.einsum('rhqk,rkhd->rqhd', probs_half, v_half)
    attended_half = attended.reshape(token_count, INNER).astype(jnp.bfloat16)
    grad_out = grad_in.reshape(token_count, D)
    grad_att = jnp.dot(grad_out, w_out.T, preferred_element_type=jnp.float32).astype(jnp.bfloat16)
    grad_heads = lax.optimization_barrier(grad_att).astype(jnp.float32).reshape(row_count, TRACE_LEN, HEADS, HEAD)
    grad_probs = jnp.einsum('rqhd,rkhd->rhqk', grad_heads, v_half)
    grad_value = jnp.einsum('rhqk,rqhd->rkhd', probs_half, grad_heads)
    weighted = lax.optimization_barrier(jnp.sum(att_probs * grad_probs, axis=-1, keepdims=True))
    grad_scores = rounded(score_gain / HEAD * att_probs * (grad_probs - weighted))
    grad_qunit = jnp.einsum('rhqk,rkhd->rqhd', grad_scores, k_half)
    grad_kunit = jnp.einsum('rhqk,rqhd->rkhd', grad_scores, q_half)
    grad_query = q_scale * (grad_qunit - q_unit * lax.optimization_barrier(jnp.mean(q_unit * grad_qunit, axis=-1, keepdims=True)))
    grad_key = k_scale * (grad_kunit - k_unit * lax.optimization_barrier(jnp.mean(k_unit * grad_kunit, axis=-1, keepdims=True)))
    dq_half = grad_query.reshape(token_count, INNER).astype(jnp.bfloat16)
    dk_half = grad_key.reshape(token_count, INNER).astype(jnp.bfloat16)
    dv_half = grad_value.reshape(token_count, INNER).astype(jnp.bfloat16)
    grad_norm = jnp.dot(dq_half, w_query.T, preferred_element_type=jnp.float32) + jnp.dot(dk_half, w_key.T, preferred_element_type=jnp.float32) + jnp.dot(dv_half, w_value.T, preferred_element_type=jnp.float32)
    grad_flat = grad_out.astype(jnp.float32) + inv_rms * (grad_norm - scaled * lax.optimization_barrier(jnp.mean(scaled * grad_norm, axis=-1, keepdims=True)))
    sums = (jnp.dot(normed.T, dq_half, preferred_element_type=jnp.float32), jnp.dot(normed.T, dk_half, preferred_element_type=jnp.float32), jnp.dot(normed.T, dv_half, preferred_element_type=jnp.float32), jnp.dot(attended_half.T, grad_out, preferred_element_type=jnp.float32))
    return (grad_flat.astype(jnp.bfloat16).reshape(rows.shape), sums)

def reference(trace_rows, upstream, counts, w_query, w_key, w_value, w_out):
    view_counts = counts.reshape(VIEWS, 1)
    is_live = jnp.arange(MOST, dtype=jnp.int32)[None, :] < view_counts
    masked = jnp.where(is_live[:, :, None, None], upstream, jnp.zeros((), upstream.dtype))
    row_blocks = trace_rows.reshape(N_GROUP * N_PEER, SLOTS, TRACE_LEN, D)
    grad_blocks = masked.reshape(N_GROUP * N_PEER, SLOTS, TRACE_LEN, D)

    def step(carry, pieces):
        block_grads, sums = row_backward(pieces[0], pieces[1], w_query, w_key, w_value, w_out)
        return (tuple((total + term for total, term in zip(carry, sums))), block_grads)
    start_sums = (jnp.zeros((D, INNER), jnp.float32), jnp.zeros((D, INNER), jnp.float32), jnp.zeros((D, INNER), jnp.float32), jnp.zeros((INNER, D), jnp.float32))
    sums, grads_all = lax.scan(step, start_sums, (row_blocks, grad_blocks))
    grad_scale = 1.0 / math.sqrt(LIVE_TOKENS)
    return (grads_all.reshape(trace_rows.shape), sums[0] * grad_scale, sums[1] * grad_scale, sums[2] * grad_scale, sums[3] * grad_scale)
```

```python
import math

import jax
import jax.numpy as jnp
from jax import lax
from jax.sharding import PartitionSpec as P

HEADS = 8


score_gain = 6.0
tiny_eps = 1e-06


def dot_rows(first_op, second_op):
    return lax.dot_general(
        first_op, second_op, (((1,), (1,)), ((), ())), preferred_element_type=jnp.float32
    )


def dot_cols(first_op, second_op):
    return lax.dot_general(
        first_op, second_op, (((0,), (0,)), ((), ())), preferred_element_type=jnp.float32
    )


def unit_heads(values):
    split_heads = values.reshape(values.shape[0], HEADS, values.shape[1] // HEADS)
    inv_scale = lax.rsqrt(jnp.mean(split_heads * split_heads, axis=-1, keepdims=True) + tiny_eps)
    return (split_heads * inv_scale, inv_scale)


def layer_backward(rows, grad_in, weights):
    w_query, w_key, w_value, w_out = weights
    row_count, row_length, feature_width = rows.shape
    token_count = row_count * row_length
    inner_width = w_query.shape[1]
    head_size = inner_width // HEADS
    flat_rows = rows.reshape(token_count, feature_width).astype(jnp.float32)
    inv_rms = lax.rsqrt(jnp.mean(flat_rows * flat_rows, axis=-1, keepdims=True) + tiny_eps)
    scaled = flat_rows * inv_rms
    normed = scaled.astype(jnp.bfloat16)
    queries = jnp.dot(normed, w_query, preferred_element_type=jnp.float32)
    keys_full = jnp.dot(normed, w_key, preferred_element_type=jnp.float32)
    values_full = jnp.dot(normed, w_value, preferred_element_type=jnp.float32)
    q_unit, q_scale = unit_heads(queries)
    k_unit, k_scale = unit_heads(keys_full)
    per_block = math.gcd(row_count, max(1, 128 // row_length))
    block_span = per_block * row_length
    block_count = token_count // block_span
    q_half = q_unit.astype(jnp.bfloat16).reshape(block_count, block_span, HEADS, head_size)
    k_half = k_unit.astype(jnp.bfloat16).reshape(block_count, block_span, HEADS, head_size)
    v_half = values_full.astype(jnp.bfloat16).reshape(block_count, block_span, HEADS, head_size)
    position = lax.iota(jnp.int32, block_span) // row_length
    same_row = position[:, None] == position[None, :]
    scores = jnp.einsum("bqhd,bkhd->bhqk", q_half, k_half, preferred_element_type=jnp.float32) * (
        score_gain / head_size
    )
    exp_scores = jnp.where(same_row, jnp.exp(scores), 0.0)
    att_probs = exp_scores / jnp.sum(exp_scores, axis=-1, keepdims=True)
    probs_half = att_probs.astype(jnp.bfloat16)
    attended = jnp.einsum("bhqk,bkhd->bqhd", probs_half, v_half, preferred_element_type=jnp.float32)
    attended_half = attended.astype(jnp.bfloat16).reshape(token_count, inner_width)
    grad_out = grad_in.reshape(token_count, feature_width)
    grad_att = dot_rows(grad_out, w_out).astype(jnp.bfloat16)
    grad_heads = grad_att.reshape(block_count, block_span, HEADS, head_size)
    grad_probs = jnp.einsum(
        "bqhd,bkhd->bhqk", grad_heads, v_half, preferred_element_type=jnp.float32
    )
    grad_value = jnp.einsum(
        "bhqk,bqhd->bkhd", probs_half, grad_heads, preferred_element_type=jnp.float32
    )
    weighted = jnp.sum(att_probs * grad_probs, axis=-1, keepdims=True)
    grad_scores = (score_gain / head_size * att_probs * (grad_probs - weighted)).astype(
        jnp.bfloat16
    )
    grad_qunit = jnp.einsum(
        "bhqk,bkhd->bqhd", grad_scores, k_half, preferred_element_type=jnp.float32
    ).reshape(token_count, HEADS, head_size)
    grad_kunit = jnp.einsum(
        "bhqk,bqhd->bkhd", grad_scores, q_half, preferred_element_type=jnp.float32
    ).reshape(token_count, HEADS, head_size)
    grad_query = q_scale * (
        grad_qunit - q_unit * jnp.mean(q_unit * grad_qunit, axis=-1, keepdims=True)
    )
    grad_key = k_scale * (
        grad_kunit - k_unit * jnp.mean(k_unit * grad_kunit, axis=-1, keepdims=True)
    )
    dq_half = grad_query.reshape(token_count, inner_width).astype(jnp.bfloat16)
    dk_half = grad_key.reshape(token_count, inner_width).astype(jnp.bfloat16)
    dv_half = grad_value.reshape(token_count, inner_width).astype(jnp.bfloat16)
    grad_norm = dot_rows(dq_half, w_query) + dot_rows(dk_half, w_key) + dot_rows(dv_half, w_value)
    grad_flat = grad_out.astype(jnp.float32) + inv_rms * (
        grad_norm - scaled * jnp.mean(scaled * grad_norm, axis=-1, keepdims=True)
    )
    saved_terms = (normed, attended_half, dq_half, dk_half, dv_half, grad_out)
    return (grad_flat.astype(jnp.bfloat16).reshape(rows.shape), saved_terms)


def grad_terms(saved_terms):
    normed, attended_half, dq_half, dk_half, dv_half, grad_out = saved_terms
    return jnp.concatenate(
        (
            dot_cols(normed, dq_half),
            dot_cols(normed, dk_half),
            dot_cols(normed, dv_half),
            dot_cols(attended_half, grad_out),
        ),
        axis=1,
    )


MESH_AXES = ("y", "core", "x", "z")
swap_pairs = [(0, 1), (1, 0)]


def spread(block, axis):
    count = lax.axis_size(axis)
    copies = jnp.broadcast_to(block[None], (count,) + block.shape)
    return lax.all_to_all(copies, axis, split_axis=0, concat_axis=0, tiled=True)


def shared_sum(blocks, axis):
    arrived = lax.all_to_all(blocks, axis, split_axis=0, concat_axis=0, tiled=True)
    return jnp.sum(arrived.astype(jnp.float32), axis=0)


def gather_weights(w_query, w_key, w_value, w_out, core):
    rows, width = w_query.shape
    both = jnp.stack(
        (
            jnp.concatenate((w_query, w_key), axis=1),
            jnp.concatenate((w_value, w_out), axis=1),
        )
    )
    half = lax.dynamic_index_in_dim(both, core, 0, keepdims=False)
    half = spread(half, "z").reshape(-1, 2 * width)
    half = spread(half, "x").reshape(-1, 2 * width)
    other = lax.ppermute(half, "core", swap_pairs)
    first = jnp.where(core == 0, half, other)
    second = jnp.where(core == 0, other, half)
    return (first[:, :width], first[:, width:], second[:, :width], second[:, width:])


def reduce_terms(first_half, second_half, core):
    mine = jnp.where(core == 0, first_half, second_half)
    theirs = jnp.where(core == 0, second_half, first_half)
    arrived = lax.ppermute(theirs.astype(jnp.bfloat16), "core", swap_pairs)
    total = (mine + arrived.astype(jnp.float32)).astype(jnp.bfloat16)
    depth, width = total.shape
    x_count, z_count = lax.axis_size("x"), lax.axis_size("z")
    total = shared_sum(total.reshape(x_count, depth // x_count, width), "x").astype(jnp.bfloat16)
    rows = depth // (x_count * z_count)
    total = shared_sum(total.reshape(z_count, rows, width), "z").astype(jnp.bfloat16)
    total = jnp.sum(spread(total, "y").astype(jnp.float32), axis=0)
    other = lax.ppermute(total, "core", swap_pairs)
    return (jnp.where(core == 0, total, other), jnp.where(core == 0, other, total))


def local(trace_rows, upstream, counts, w_query, w_key, w_value, w_out):
    core = lax.axis_index("core")
    weights = gather_weights(w_query, w_key, w_value, w_out, core)
    view_count, most_rows, row_length, feature_width = trace_rows.shape
    view_counts = counts.reshape(view_count)
    is_live = lax.iota(jnp.int32, most_rows)[None, :] < view_counts[:, None]
    masked = jnp.where(is_live[:, :, None, None], upstream, jnp.zeros((), upstream.dtype))
    slot_count = view_count * most_rows
    slot_shape = (slot_count, row_length, feature_width)
    done_rows, saved_terms = layer_backward(
        trace_rows.reshape(slot_shape), masked.reshape(slot_shape), weights
    )
    terms = grad_terms(saved_terms)
    first, second = reduce_terms(
        terms[:, : 2 * feature_width], terms[:, 2 * feature_width :], core
    )
    devices = math.prod(lax.axis_size(name) for name in MESH_AXES)
    grad_scale = 1.0 / math.sqrt(devices * (slot_count // 2) * row_length)
    first, second = first * grad_scale, second * grad_scale
    return (
        done_rows.reshape(trace_rows.shape),
        first[:, :feature_width],
        first[:, feature_width:],
        second[:, :feature_width],
        second[:, feature_width:],
    )


def solution(mesh):
    fine_mesh = jax.sharding.Mesh(mesh.devices.reshape(8, 2, 4, 8), MESH_AXES)
    every, peer = P(MESH_AXES), P(("x", "z"), None)
    in_specs = (every, every, P(("y", "core"), ("x", "z")), peer, peer, peer, peer)
    out_specs = (every, peer, peer, peer, peer)
    return jax.shard_map(
        local, mesh=fine_mesh, in_specs=in_specs, out_specs=out_specs, check_vma=False
    )
```

```python
import math

import jax
import jax.numpy as jnp
from jax import lax
from jax.sharding import PartitionSpec as P

HEADS = 8


score_gain = 6.0
tiny_eps = 1e-06


def dot_rows(first_op, second_op):
    return lax.dot_general(
        first_op, second_op, (((1,), (1,)), ((), ())), preferred_element_type=jnp.float32
    )


def dot_cols(first_op, second_op):
    return lax.dot_general(
        first_op, second_op, (((0,), (0,)), ((), ())), preferred_element_type=jnp.float32
    )


def unit_heads(values):
    split_heads = values.reshape(values.shape[0], HEADS, values.shape[1] // HEADS)
    inv_scale = lax.rsqrt(jnp.mean(split_heads * split_heads, axis=-1, keepdims=True) + tiny_eps)
    return (split_heads * inv_scale, inv_scale)


def layer_backward(rows, grad_in, weights):
    w_query, w_key, w_value, w_out = weights
    row_count, row_length, feature_width = rows.shape
    token_count = row_count * row_length
    inner_width = w_query.shape[1]
    head_size = inner_width // HEADS
    flat_rows = rows.reshape(token_count, feature_width).astype(jnp.float32)
    inv_rms = lax.rsqrt(jnp.mean(flat_rows * flat_rows, axis=-1, keepdims=True) + tiny_eps)
    scaled = flat_rows * inv_rms
    normed = scaled.astype(jnp.bfloat16)
    queries = jnp.dot(normed, w_query, preferred_element_type=jnp.float32)
    keys_full = jnp.dot(normed, w_key, preferred_element_type=jnp.float32)
    values_full = jnp.dot(normed, w_value, preferred_element_type=jnp.float32)
    q_unit, q_scale = unit_heads(queries)
    k_unit, k_scale = unit_heads(keys_full)
    per_block = math.gcd(row_count, max(1, 128 // row_length))
    block_span = per_block * row_length
    block_count = token_count // block_span
    q_half = q_unit.astype(jnp.bfloat16).reshape(block_count, block_span, HEADS, head_size)
    k_half = k_unit.astype(jnp.bfloat16).reshape(block_count, block_span, HEADS, head_size)
    v_half = values_full.astype(jnp.bfloat16).reshape(block_count, block_span, HEADS, head_size)
    position = lax.iota(jnp.int32, block_span) // row_length
    same_row = position[:, None] == position[None, :]
    scores = jnp.einsum("bqhd,bkhd->bhqk", q_half, k_half, preferred_element_type=jnp.float32) * (
        score_gain / head_size
    )
    exp_scores = jnp.where(same_row, jnp.exp(scores), 0.0)
    att_probs = exp_scores / jnp.sum(exp_scores, axis=-1, keepdims=True)
    probs_half = att_probs.astype(jnp.bfloat16)
    attended = jnp.einsum("bhqk,bkhd->bqhd", probs_half, v_half, preferred_element_type=jnp.float32)
    attended_half = attended.astype(jnp.bfloat16).reshape(token_count, inner_width)
    grad_out = grad_in.reshape(token_count, feature_width)
    grad_att = dot_rows(grad_out, w_out).astype(jnp.bfloat16)
    grad_heads = grad_att.reshape(block_count, block_span, HEADS, head_size)
    grad_probs = jnp.einsum(
        "bqhd,bkhd->bhqk", grad_heads, v_half, preferred_element_type=jnp.float32
    )
    grad_value = jnp.einsum(
        "bhqk,bqhd->bkhd", probs_half, grad_heads, preferred_element_type=jnp.float32
    )
    weighted = jnp.sum(att_probs * grad_probs, axis=-1, keepdims=True)
    grad_scores = (score_gain / head_size * att_probs * (grad_probs - weighted)).astype(
        jnp.bfloat16
    )
    grad_qunit = jnp.einsum(
        "bhqk,bkhd->bqhd", grad_scores, k_half, preferred_element_type=jnp.float32
    ).reshape(token_count, HEADS, head_size)
    grad_kunit = jnp.einsum(
        "bhqk,bqhd->bkhd", grad_scores, q_half, preferred_element_type=jnp.float32
    ).reshape(token_count, HEADS, head_size)
    grad_query = q_scale * (
        grad_qunit - q_unit * jnp.mean(q_unit * grad_qunit, axis=-1, keepdims=True)
    )
    grad_key = k_scale * (
        grad_kunit - k_unit * jnp.mean(k_unit * grad_kunit, axis=-1, keepdims=True)
    )
    dq_half = grad_query.reshape(token_count, inner_width).astype(jnp.bfloat16)
    dk_half = grad_key.reshape(token_count, inner_width).astype(jnp.bfloat16)
    dv_half = grad_value.reshape(token_count, inner_width).astype(jnp.bfloat16)
    grad_norm = dot_rows(dq_half, w_query) + dot_rows(dk_half, w_key) + dot_rows(dv_half, w_value)
    grad_flat = grad_out.astype(jnp.float32) + inv_rms * (
        grad_norm - scaled * jnp.mean(scaled * grad_norm, axis=-1, keepdims=True)
    )
    saved_terms = (normed, attended_half, dq_half, dk_half, dv_half, grad_out)
    return (grad_flat.astype(jnp.bfloat16).reshape(rows.shape), saved_terms)


def grad_terms(saved_terms):
    normed, attended_half, dq_half, dk_half, dv_half, grad_out = saved_terms
    return jnp.concatenate(
        (
            dot_cols(normed, dq_half),
            dot_cols(normed, dk_half),
            dot_cols(normed, dv_half),
            dot_cols(attended_half, grad_out),
        ),
        axis=1,
    )


MESH_AXES = ("y", "core", "x", "z")
swap_pairs = [(0, 1), (1, 0)]


def spread(block, axis):
    count = lax.axis_size(axis)
    copies = jnp.broadcast_to(block[None], (count,) + block.shape)
    return lax.all_to_all(copies, axis, split_axis=0, concat_axis=0, tiled=True)


def shared_sum(blocks, axis):
    arrived = lax.all_to_all(blocks, axis, split_axis=0, concat_axis=0, tiled=True)
    return jnp.sum(arrived.astype(jnp.float32), axis=0)


def gather_weights(w_query, w_key, w_value, w_out, core):
    rows, width = w_query.shape
    both = jnp.stack(
        (
            jnp.concatenate((w_query, w_key), axis=1),
            jnp.concatenate((w_value, w_out), axis=1),
        )
    )
    half = lax.dynamic_index_in_dim(both, core, 0, keepdims=False)
    half = spread(half, ("x", "z")).reshape(-1, 2 * width)
    other = lax.ppermute(half, "core", swap_pairs)
    first = jnp.where(core == 0, half, other)
    second = jnp.where(core == 0, other, half)
    return (first[:, :width], first[:, width:], second[:, :width], second[:, width:])


def reduce_terms(first_half, second_half, core):
    mine = jnp.where(core == 0, first_half, second_half)
    theirs = jnp.where(core == 0, second_half, first_half)
    arrived = lax.ppermute(theirs.astype(jnp.bfloat16), "core", swap_pairs)
    total = (mine + arrived.astype(jnp.float32)).astype(jnp.bfloat16)
    depth, width = total.shape
    peers = lax.axis_size(("x", "z"))
    total = shared_sum(total.reshape(peers, depth // peers, width), ("x", "z"))
    total = jnp.sum(spread(total.astype(jnp.bfloat16), "y").astype(jnp.float32), axis=0)
    other = lax.ppermute(total, "core", swap_pairs)
    return (jnp.where(core == 0, total, other), jnp.where(core == 0, other, total))


def local(trace_rows, upstream, counts, w_query, w_key, w_value, w_out):
    core = lax.axis_index("core")
    weights = gather_weights(w_query, w_key, w_value, w_out, core)
    view_count, most_rows, row_length, feature_width = trace_rows.shape
    view_counts = counts.reshape(view_count)
    is_live = lax.iota(jnp.int32, most_rows)[None, :] < view_counts[:, None]
    masked = jnp.where(is_live[:, :, None, None], upstream, jnp.zeros((), upstream.dtype))
    slot_count = view_count * most_rows
    slot_shape = (slot_count, row_length, feature_width)
    done_rows, saved_terms = layer_backward(
        trace_rows.reshape(slot_shape), masked.reshape(slot_shape), weights
    )
    terms = grad_terms(saved_terms)
    first, second = reduce_terms(
        terms[:, : 2 * feature_width], terms[:, 2 * feature_width :], core
    )
    devices = math.prod(lax.axis_size(name) for name in MESH_AXES)
    grad_scale = 1.0 / math.sqrt(devices * (slot_count // 2) * row_length)
    first, second = first * grad_scale, second * grad_scale
    return (
        done_rows.reshape(trace_rows.shape),
        first[:, :feature_width],
        first[:, feature_width:],
        second[:, :feature_width],
        second[:, feature_width:],
    )


def solution(mesh):
    fine_mesh = jax.sharding.Mesh(mesh.devices.reshape(8, 2, 4, 8), MESH_AXES)
    every, peer = P(MESH_AXES), P(("x", "z"), None)
    in_specs = (every, every, P(("y", "core"), ("x", "z")), peer, peer, peer, peer)
    out_specs = (every, peer, peer, peer, peer)
    return jax.shard_map(
        local, mesh=fine_mesh, in_specs=in_specs, out_specs=out_specs, check_vma=False
    )
```

```python
import math
import jax
import jax.numpy as jnp
from jax import lax
from jax.experimental import pallas as pl
from jax.experimental.pallas import tpu as pltpu
from jax.sharding import PartitionSpec as P

HEADS = 8
HEAD = 64
ROW = 32
SPAN = 128
STEP = 256
gain = 6.0 / HEAD
tiny_eps = 1e-06
f32, bf16 = jnp.float32, jnp.bfloat16


def dot_nn(a, b):
    return lax.dot_general(a, b, (((1,), (0,)), ((), ())), preferred_element_type=f32)


def dot_nt(a, b):
    return lax.dot_general(a, b, (((1,), (1,)), ((), ())), preferred_element_type=f32)


def dot_tn(a, b):
    return lax.dot_general(a, b, (((0,), (0,)), ((), ())), preferred_element_type=f32)


def head_ones(width):
    row = lax.broadcasted_iota(jnp.int32, (width, width), 0) // HEAD
    col = lax.broadcasted_iota(jnp.int32, (width, width), 1) // HEAD
    return jnp.where(row == col, 1.0, 0.0).astype(bf16)


def head_means(values, ones):
    return dot_nn(values.astype(bf16), ones) * (1.0 / HEAD)


def stacked(block):
    first = lax.broadcasted_iota(jnp.int32, block.shape, 1) < HEAD
    zero = jnp.zeros((), block.dtype)
    return jnp.concatenate((jnp.where(first, block, zero), jnp.where(first, zero, block)), axis=0)


def unstacked(block):
    span = block.shape[0] // 2
    first = lax.broadcasted_iota(jnp.int32, (span, block.shape[1]), 1) < HEAD
    return jnp.where(first, block[:span], block[span:])


def per_head(values, scale_of):
    return jnp.concatenate(
        (scale_of(values[:, :SPAN]), scale_of(values[:, SPAN:])), axis=1
    )


def forward_kernel(normed_ref, grads_ref, wqkv_ref, raw_ref, half_ref, probs_ref, dwo_ref, acc_ref):
    step = pl.program_id(0)
    width = dwo_ref.shape[0]
    ones = head_ones(width)
    qkv = dot_nn(normed_ref[...], wqkv_ref[...])
    query, key = qkv[:, :width], qkv[:, width : 2 * width]
    raw_ref[...] = qkv[:, : 2 * width]
    q_half = (query * lax.rsqrt(head_means(query * query, ones) + tiny_eps)).astype(bf16)
    k_half = (key * lax.rsqrt(head_means(key * key, ones) + tiny_eps)).astype(bf16)
    v_half = qkv[:, 2 * width :].astype(bf16)
    half_ref[:, :width] = q_half
    half_ref[:, width : 2 * width] = k_half
    half_ref[:, 2 * width :] = v_half
    row_of = lax.broadcasted_iota(jnp.int32, (SPAN, 2 * SPAN), 0) // ROW
    col_of = lax.broadcasted_iota(jnp.int32, (SPAN, 2 * SPAN), 1) % SPAN // ROW
    same_row = row_of == col_of
    spans = []
    for low in range(0, STEP, SPAN):
        pairs = []
        for left in range(0, width, 2 * HEAD):
            rows, cols = slice(low, low + SPAN), slice(left, left + 2 * HEAD)
            k_two, v_two = stacked(k_half[rows, cols]), stacked(v_half[rows, cols])
            scores = dot_nt(q_half[rows, cols], k_two)
            exps = jnp.where(same_row, jnp.exp(scores * gain), 0.0)
            probs = per_head(exps, lambda e: e * (1.0 / jnp.sum(e, axis=1, keepdims=True)))
            probs_ref[rows, 2 * left : 2 * left + 2 * SPAN] = probs
            pairs.append(dot_nn(probs.astype(bf16), v_two).astype(bf16))
        spans.append(jnp.concatenate(pairs, axis=1))
    attended = jnp.concatenate(spans, axis=0)
    term = dot_tn(attended, grads_ref[...])

    @pl.when(step == 0)
    def _():
        acc_ref[...] = term

    @pl.when(step > 0)
    def _():
        acc_ref[...] += term

    @pl.when(step == pl.num_programs(0) - 1)
    def _():
        dwo_ref[...] = acc_ref[...].astype(bf16)


def backward_kernel(
    normed_ref, grads_ref, raw_ref, half_ref, probs_ref, wo_ref, dqkv_ref, dw_ref, acc_ref
):
    step = pl.program_id(0)
    width = wo_ref.shape[0]
    ones = head_ones(width)
    grad_att = dot_nt(grads_ref[...], wo_ref[...]).astype(bf16)
    spans = []
    for low in range(0, STEP, SPAN):
        d_query, d_key, d_value = [], [], []
        for left in range(0, width, 2 * HEAD):
            rows, cols = slice(low, low + SPAN), slice(left, left + 2 * HEAD)
            q_pair = half_ref[rows, left : left + 2 * HEAD]
            k_two = stacked(half_ref[rows, width + left : width + left + 2 * HEAD])
            v_two = stacked(half_ref[rows, 2 * width + left : 2 * width + left + 2 * HEAD])
            g_pair = grad_att[rows, cols]
            probs = probs_ref[rows, 2 * left : 2 * left + 2 * SPAN]
            grad_probs = dot_nt(g_pair, v_two)
            d_value.append(unstacked(dot_tn(probs.astype(bf16), g_pair)))
            weighted = probs * grad_probs
            d_scores = jnp.concatenate(
                [
                    weighted[:, half]
                    - probs[:, half] * jnp.sum(weighted[:, half], axis=1, keepdims=True)
                    for half in (slice(0, SPAN), slice(SPAN, 2 * SPAN))
                ],
                axis=1,
            )
            d_scores = (d_scores * gain).astype(bf16)
            d_query.append(dot_nn(d_scores, k_two))
            d_key.append(unstacked(dot_tn(d_scores, q_pair)))
        spans.append([jnp.concatenate(part, axis=1) for part in (d_query, d_key, d_value)])
    d_query, d_key, d_value = (jnp.concatenate(part, axis=0) for part in zip(*spans))

    def through_norm(raw, grad):
        scale = lax.rsqrt(head_means(raw * raw, ones) + tiny_eps)
        unit = raw * scale
        return (scale * (grad - unit * head_means(unit * grad, ones))).astype(bf16)

    dqkv = jnp.concatenate(
        (
            through_norm(raw_ref[:, :width], d_query),
            through_norm(raw_ref[:, width:], d_key),
            d_value.astype(bf16),
        ),
        axis=1,
    )
    dqkv_ref[...] = dqkv
    term = dot_tn(normed_ref[...], dqkv)

    @pl.when(step == 0)
    def _():
        acc_ref[...] = term

    @pl.when(step > 0)
    def _():
        acc_ref[...] += term

    @pl.when(step == pl.num_programs(0) - 1)
    def _():
        dw_ref[...] = acc_ref[...].astype(bf16)


def token_spec(width):
    return pl.BlockSpec((STEP, width), lambda i: (i, 0))


def whole_spec(shape):
    return pl.BlockSpec(shape, lambda i: (0, 0))


def forward(normed, grads, wqkv):
    tokens, depth = normed.shape
    width = wqkv.shape[1] // 3
    return pl.pallas_call(
        forward_kernel,
        grid=(tokens // STEP,),
        in_specs=[token_spec(depth), token_spec(depth), whole_spec(wqkv.shape)],
        out_specs=[
            token_spec(2 * width),
            token_spec(3 * width),
            token_spec(2 * width),
            whole_spec((width, depth)),
        ],
        out_shape=[
            jax.ShapeDtypeStruct((tokens, 2 * width), f32),
            jax.ShapeDtypeStruct((tokens, 3 * width), bf16),
            jax.ShapeDtypeStruct((tokens, 2 * width), f32),
            jax.ShapeDtypeStruct((width, depth), bf16),
        ],
        scratch_shapes=[pltpu.VMEM((width, depth), f32)],
        compiler_params=pltpu.CompilerParams(vmem_limit_bytes=32 * 1024 * 1024),
        cost_estimate=pl.CostEstimate(
            flops=3 * tokens * depth * width * 3, bytes_accessed=8 << 20, transcendentals=0
        ),
        name="attention_forward",
    )(normed, grads, wqkv)


def backward(normed, grads, raw, half, probs, wo):
    tokens, depth = normed.shape
    width = wo.shape[0]
    return pl.pallas_call(
        backward_kernel,
        grid=(tokens // STEP,),
        in_specs=[
            token_spec(depth),
            token_spec(depth),
            token_spec(2 * width),
            token_spec(3 * width),
            token_spec(2 * width),
            whole_spec(wo.shape),
        ],
        out_specs=[token_spec(3 * width), whole_spec((depth, 3 * width))],
        out_shape=[
            jax.ShapeDtypeStruct((tokens, 3 * width), bf16),
            jax.ShapeDtypeStruct((depth, 3 * width), bf16),
        ],
        scratch_shapes=[pltpu.VMEM((depth, 3 * width), f32)],
        compiler_params=pltpu.CompilerParams(vmem_limit_bytes=32 * 1024 * 1024),
        cost_estimate=pl.CostEstimate(
            flops=6 * tokens * depth * width * 3, bytes_accessed=8 << 20, transcendentals=0
        ),
        name="attention_backward",
    )(normed, grads, raw, half, probs, wo)


MESH_AXES = ("y", "core", "x", "z")
PEERS = ("x", "z")


def swapped(block):
    return lax.ppermute(block, "core", [(0, 1), (1, 0)])


def spread(block, axis):
    copies = jnp.broadcast_to(block[None], (lax.axis_size(axis),) + block.shape)
    return lax.all_to_all(copies, axis, split_axis=0, concat_axis=0, tiled=True)


def shared_sum(blocks, axis):
    arrived = lax.all_to_all(blocks, axis, split_axis=0, concat_axis=0, tiled=True)
    return jnp.sum(arrived.astype(f32), axis=0)


def local(trace_rows, upstream, counts, w_query, w_key, w_value, w_out):
    core = lax.axis_index("core")
    is_first = core == 0
    view_count, most_rows, row_length, depth = trace_rows.shape
    tokens = view_count * most_rows * row_length
    half_width = w_query.shape[1] // 2
    own = core * half_width

    def ordered(mine, theirs, axis):
        return jnp.concatenate(
            (jnp.where(is_first, mine, theirs), jnp.where(is_first, theirs, mine)), axis=axis
        )

    def half_of(block, axis, of_other=False):
        low = half_width - own if of_other else own
        return lax.dynamic_slice_in_dim(block, low, half_width, axis)

    shards = jnp.concatenate(
        [half_of(weight, 1) for weight in (w_query, w_key, w_value, w_out)], axis=1
    )
    gathered = spread(shards, PEERS).reshape(-1, 4 * half_width)
    w_qkv, w_out_cols = gathered[:, : 3 * half_width], gathered[:, 3 * half_width :]
    w_out_rows = ordered(
        half_of(w_out_cols, 0), swapped(half_of(w_out_cols, 0, of_other=True)), 1
    )

    is_live = lax.iota(jnp.int32, most_rows)[None, :] < counts.reshape(view_count)[:, None]
    masked = jnp.where(is_live[:, :, None, None], upstream, jnp.zeros((), upstream.dtype))
    rows, grads = trace_rows.reshape(tokens, depth), masked.reshape(tokens, depth)
    both_rows = jnp.concatenate((rows, swapped(rows)), axis=0).astype(f32)
    both_grads = jnp.concatenate((grads, swapped(grads)), axis=0)
    inv_rms = lax.rsqrt(jnp.mean(both_rows * both_rows, axis=-1, keepdims=True) + tiny_eps)
    normed = (both_rows * inv_rms).astype(bf16)

    raw, half, probs, d_out_rows = forward(normed, both_grads, w_qkv)
    d_out_cols = ordered(
        half_of(d_out_rows, 1), swapped(half_of(d_out_rows, 1, of_other=True)), 0
    )
    d_qkv, d_weights = backward(normed, both_grads, raw, half, probs, w_out_rows)

    terms = jnp.concatenate((d_weights, d_out_cols), axis=1)
    peers = lax.axis_size(PEERS)
    total = shared_sum(terms.reshape(peers, depth // peers, 4 * half_width), PEERS)
    total = jnp.sum(spread(total.astype(bf16), "y").astype(f32), axis=0)
    devices = math.prod(lax.axis_size(name) for name in MESH_AXES)
    total = total * (1.0 / math.sqrt(devices * tokens // 2))
    other_total = swapped(total)
    weight_grads = [
        ordered(total[:, low : low + half_width], other_total[:, low : low + half_width], 1)
        for low in range(0, 4 * half_width, half_width)
    ]

    grad_norm = dot_nt(d_qkv, w_qkv)
    grad_norm = grad_norm[:tokens] + swapped(grad_norm[tokens:].astype(bf16)).astype(f32)
    inv_rms, scaled = inv_rms[:tokens], both_rows[:tokens] * inv_rms[:tokens]
    done = grads.astype(f32) + inv_rms * (
        grad_norm - scaled * jnp.mean(scaled * grad_norm, axis=-1, keepdims=True)
    )
    return (done.astype(bf16).reshape(trace_rows.shape), *weight_grads)


def solution(mesh):
    fine_mesh = jax.sharding.Mesh(mesh.devices.reshape(8, 2, 4, 8), MESH_AXES)
    every, peer = P(MESH_AXES), P(PEERS, None)
    in_specs = (every, every, P(("y", "core"), PEERS), peer, peer, peer, peer)
    out_specs = (every, peer, peer, peer, peer)
    return jax.shard_map(
        local, mesh=fine_mesh, in_specs=in_specs, out_specs=out_specs, check_vma=False
    )
```

```python
import math
import jax
import jax.numpy as jnp
from jax import lax
from jax.experimental import pallas as pl
from jax.experimental.pallas import tpu as pltpu
from jax.sharding import PartitionSpec as P

HEAD = 64
ROW = 32
SPAN = 128
gain = 6.0 / HEAD
tiny_eps = 1e-06
f32, bf16 = jnp.float32, jnp.bfloat16


def dot_nn(a, b):
    return lax.dot_general(a, b, (((1,), (0,)), ((), ())), preferred_element_type=f32)


def dot_nt(a, b):
    return lax.dot_general(a, b, (((1,), (1,)), ((), ())), preferred_element_type=f32)


def dot_tn(a, b):
    return lax.dot_general(a, b, (((0,), (0,)), ((), ())), preferred_element_type=f32)


def head_ones(width):
    row = lax.broadcasted_iota(jnp.int32, (width, width), 0) // HEAD
    col = lax.broadcasted_iota(jnp.int32, (width, width), 1) // HEAD
    return jnp.where(row == col, 1.0, 0.0).astype(bf16)


def head_means(values, ones):
    return dot_nn(values.astype(bf16), ones) * (1.0 / HEAD)


def stacked(block):
    first = lax.broadcasted_iota(jnp.int32, block.shape, 1) < HEAD
    zero = jnp.zeros((), block.dtype)
    return jnp.concatenate((jnp.where(first, block, zero), jnp.where(first, zero, block)), axis=0)


def unstacked(block):
    span = block.shape[0] // 2
    first = lax.broadcasted_iota(jnp.int32, (span, block.shape[1]), 1) < HEAD
    return jnp.where(first, block[:span], block[span:])


def attention(q_half, k_half, v_half, grad_att, same_row):
    k_two, v_two = stacked(k_half), stacked(v_half)
    exps = jnp.where(same_row, jnp.exp(dot_nt(q_half, k_two) * gain), 0.0)
    grad_probs = dot_nt(grad_att, v_two)
    probs, d_scores = [], []
    for half in (slice(0, SPAN), slice(SPAN, 2 * SPAN)):
        part = exps[:, half] * (1.0 / jnp.sum(exps[:, half], axis=1, keepdims=True))
        weighted = part * grad_probs[:, half]
        total = jnp.sum(weighted, axis=1, keepdims=True)
        probs.append(part.astype(bf16))
        d_scores.append(((weighted - part * total) * gain).astype(bf16))
    probs, d_scores = jnp.concatenate(probs, axis=1), jnp.concatenate(d_scores, axis=1)
    return (
        dot_nn(probs, v_two).astype(bf16),
        dot_nn(d_scores, k_two),
        unstacked(dot_tn(d_scores, q_half)),
        unstacked(dot_tn(probs, grad_att)).astype(bf16),
    )


def layer_kernel(
    core_ref, counts_ref, rows_ref, up_ref, mine_ref, theirs_ref,
    d_mine_ref, d_theirs_ref, out_mine_ref, out_theirs_ref,
    normed_ref, masked_ref, att_ref,
):
    step = pl.program_id(0)
    tokens = rows_ref.shape[0]
    width = mine_ref.shape[1] // 4
    own = pl.multiple_of(core_ref[0] * width, width)
    other = pl.multiple_of(width - own, width)
    here = pl.ds(pl.multiple_of(step * tokens, tokens), tokens)
    ones = head_ones(width)

    rows = rows_ref[...].astype(f32)
    inv_rms = lax.rsqrt(jnp.mean(rows * rows, axis=1, keepdims=True) + tiny_eps)
    normed = (rows * inv_rms).astype(bf16)
    normed_ref[here, :] = normed
    slot = lax.broadcasted_iota(jnp.int32, up_ref.shape, 0) // ROW
    masked_ref[here, :] = jnp.where(slot < counts_ref[step], up_ref[...], jnp.zeros((), bf16))

    row_of = lax.broadcasted_iota(jnp.int32, (SPAN, 2 * SPAN), 0) // ROW
    col_of = lax.broadcasted_iota(jnp.int32, (SPAN, 2 * SPAN), 1) % SPAN // ROW
    same_row = row_of == col_of

    for weight_ref, d_ref, heads, place in (
        (theirs_ref, d_theirs_ref, other, 1),
        (mine_ref, d_mine_ref, own, 0),
    ):
        qkv = dot_nn(normed, weight_ref[:, : 3 * width])
        query, key = qkv[:, :width], qkv[:, width : 2 * width]
        q_scale = lax.rsqrt(head_means(query * query, ones) + tiny_eps)
        k_scale = lax.rsqrt(head_means(key * key, ones) + tiny_eps)
        q_unit, k_unit = query * q_scale, key * k_scale
        q_half, k_half = q_unit.astype(bf16), k_unit.astype(bf16)
        v_half = qkv[:, 2 * width :].astype(bf16)
        grad_att = (
            dot_nt(masked_ref[here, pl.ds(own, width)], mine_ref[pl.ds(heads, width), 3 * width :])
            + dot_nt(
                masked_ref[here, pl.ds(other, width)], theirs_ref[pl.ds(heads, width), 3 * width :]
            )
        ).astype(bf16)
        spans = []
        for low in range(0, tokens, SPAN):
            pairs = []
            for left in range(0, width, 2 * HEAD):
                at = (slice(low, low + SPAN), slice(left, left + 2 * HEAD))
                pairs.append(
                    attention(q_half[at], k_half[at], v_half[at], grad_att[at], same_row)
                )
            spans.append([jnp.concatenate(part, axis=1) for part in zip(*pairs)])
        attended, d_query, d_key, d_value = (
            jnp.concatenate(part, axis=0) for part in zip(*spans)
        )
        att_ref[here, place * width : (place + 1) * width] = attended
        d_ref[here, :width] = (
            q_scale * (d_query - q_unit * head_means(q_unit * d_query, ones))
        ).astype(bf16)
        d_ref[here, width : 2 * width] = (
            k_scale * (d_key - k_unit * head_means(k_unit * d_key, ones))
        ).astype(bf16)
        d_ref[here, 2 * width :] = d_value

    @pl.when(step == pl.num_programs(0) - 1)
    def _():
        for d_ref, out_ref, cols in (
            (d_theirs_ref, out_theirs_ref, other),
            (d_mine_ref, out_mine_ref, own),
        ):
            out_ref[:, : 3 * width] = dot_tn(normed_ref[...], d_ref[...]).astype(bf16)
            grads = masked_ref[:, pl.ds(cols, width)]
            for heads, place in ((own, 0), (other, 1)):
                part = att_ref[:, place * width : (place + 1) * width]
                out_ref[pl.ds(heads, width), 3 * width :] = dot_tn(part, grads).astype(bf16)


def layer(core, counts, rows, up, mine, theirs):
    tokens, depth = rows.shape
    views = counts.shape[0]
    width = mine.shape[1] // 4
    smem = pl.BlockSpec(memory_space=pltpu.SMEM)
    part = pl.BlockSpec((tokens // views, depth), lambda i: (i, 0))

    def whole(shape):
        return pl.BlockSpec(shape, lambda i: (0, 0))

    outs = [(tokens, 3 * width)] * 2 + [(depth, 4 * width)] * 2
    return pl.pallas_call(
        layer_kernel,
        grid=(views,),
        in_specs=[smem, smem, part, part, whole(mine.shape), whole(theirs.shape)],
        out_specs=[whole(shape) for shape in outs],
        out_shape=[jax.ShapeDtypeStruct(shape, bf16) for shape in outs],
        scratch_shapes=[pltpu.VMEM((tokens, depth), bf16)] * 3,
        compiler_params=pltpu.CompilerParams(vmem_limit_bytes=40 * 1024 * 1024),
        cost_estimate=pl.CostEstimate(
            flops=20 * tokens * depth * depth, bytes_accessed=6 << 20, transcendentals=0
        ),
        name="attention_layer",
    )(core, counts, rows, up, mine, theirs)


MESH_AXES = ("y", "core", "x", "z")
PEERS = ("x", "z")


def swapped(block):
    return lax.ppermute(block, "core", [(0, 1), (1, 0)])


def sent(blocks, axis):
    return lax.all_to_all(blocks, axis, split_axis=0, concat_axis=0, tiled=True)


def shared_sum(terms, axis):
    count = lax.axis_size(axis)
    blocks = terms.reshape(count, terms.shape[0] // count, terms.shape[1])
    return jnp.sum(sent(blocks, axis).astype(f32), axis=0).astype(bf16)


def copies_kernel(core_ref, *refs):
    *weight_refs, out_ref = refs
    width = weight_refs[0].shape[1] // 2
    own = pl.multiple_of(core_ref[0] * width, width)
    for index, weight_ref in enumerate(weight_refs):
        block = weight_ref[:, pl.ds(own, width)]
        out_ref[:, :, index * width : (index + 1) * width] = jnp.broadcast_to(
            block[None], (out_ref.shape[0],) + block.shape
        )


def weight_copies(core, weights, count):
    rows, width = weights[0].shape
    parts = 4
    out = (count, rows, 2 * width)
    return pl.pallas_call(
        copies_kernel,
        grid=(parts,),
        in_specs=[pl.BlockSpec(memory_space=pltpu.SMEM)]
        + [pl.BlockSpec((rows, width), lambda i: (0, 0))] * 4,
        out_specs=pl.BlockSpec((count // parts,) + out[1:], lambda i: (i, 0, 0)),
        out_shape=jax.ShapeDtypeStruct(out, bf16),
        name="weight_copies",
    )(core, *weights)


def split_kernel(core_ref, mine_ref, theirs_ref, *out_refs):
    width = mine_ref.shape[1] // 4
    own = pl.multiple_of(core_ref[0] * width, width)
    other = pl.multiple_of(width - own, width)
    for index, out_ref in enumerate(out_refs):
        cols = slice(index * width, (index + 1) * width)
        out_ref[:, pl.ds(own, width)] = mine_ref[:, cols]
        out_ref[:, pl.ds(other, width)] = theirs_ref[:, cols]


def split_weights(core, mine, theirs):
    rows, width = mine.shape
    vmem = pl.BlockSpec(memory_space=pltpu.VMEM)
    return pl.pallas_call(
        split_kernel,
        in_specs=[pl.BlockSpec(memory_space=pltpu.SMEM), vmem, vmem],
        out_specs=[vmem] * 4,
        out_shape=[jax.ShapeDtypeStruct((rows, width // 2), f32)] * 4,
        name="split_weights",
    )(core, mine, theirs)


def local(trace_rows, upstream, counts, w_query, w_key, w_value, w_out):
    core = lax.axis_index("core").reshape(1)
    view_count, most_rows, row_length, depth = trace_rows.shape
    tokens = view_count * most_rows * row_length
    view_counts = counts.reshape(view_count)

    copies = weight_copies(core, (w_query, w_key, w_value, w_out), lax.axis_size(PEERS))
    mine = sent(copies, PEERS).reshape(depth, -1)
    theirs = swapped(mine)

    rows, up = trace_rows.reshape(tokens, depth), upstream.reshape(tokens, depth)
    d_mine, d_theirs, out_mine, out_theirs = layer(core, view_counts, rows, up, mine, theirs)

    terms = out_mine.astype(f32) + swapped(out_theirs).astype(f32)
    total = shared_sum(shared_sum(terms.astype(bf16), "x"), "z")
    spread = jnp.broadcast_to(total[None], (lax.axis_size("y"),) + total.shape)
    total = jnp.sum(sent(spread, "y").astype(f32), axis=0)
    devices = math.prod(lax.axis_size(name) for name in MESH_AXES)
    total = total * (1.0 / math.sqrt(devices * tokens // 2))
    weight_grads = split_weights(core, total, swapped(total))

    used = d_mine.shape[1]
    grad_norm = dot_nt(d_mine, mine[:, :used]) + dot_nt(d_theirs, theirs[:, :used])
    rows = rows.astype(f32)
    inv_rms = lax.rsqrt(jnp.mean(rows * rows, axis=-1, keepdims=True) + tiny_eps)
    scaled = rows * inv_rms
    is_live = lax.iota(jnp.int32, most_rows)[None, :] < view_counts[:, None]
    is_live = jnp.repeat(is_live.reshape(-1), row_length)[:, None]
    masked = jnp.where(is_live, up, jnp.zeros((), up.dtype)).astype(f32)
    done = masked + inv_rms * (
        grad_norm - scaled * jnp.mean(scaled * grad_norm, axis=-1, keepdims=True)
    )
    return (done.astype(bf16).reshape(trace_rows.shape), *weight_grads)


def solution(mesh):
    fine_mesh = jax.sharding.Mesh(mesh.devices.reshape(8, 2, 4, 8), MESH_AXES)
    every, peer = P(MESH_AXES), P(PEERS, None)
    in_specs = (every, every, P(("y", "core"), PEERS), peer, peer, peer, peer)
    out_specs = (every, peer, peer, peer, peer)
    return jax.shard_map(
        local, mesh=fine_mesh, in_specs=in_specs, out_specs=out_specs, check_vma=False
    )
```

```python
import functools
import math
import jax
import jax.numpy as jnp
from jax import lax
from jax.experimental import pallas as pl
from jax.experimental.pallas import tpu as pltpu
from jax.sharding import PartitionSpec as P

HEAD = 64
ROW = 32
SPAN = 128
gain = 6.0 / HEAD
tiny_eps = 1e-06
f32, bf16 = jnp.float32, jnp.bfloat16


def dot_nn(a, b):
    return lax.dot_general(a, b, (((1,), (0,)), ((), ())), preferred_element_type=f32)


def dot_nt(a, b):
    return lax.dot_general(a, b, (((1,), (1,)), ((), ())), preferred_element_type=f32)


def dot_tn(a, b):
    return lax.dot_general(a, b, (((0,), (0,)), ((), ())), preferred_element_type=f32)


def head_ones(width):
    row = lax.broadcasted_iota(jnp.int32, (width, width), 0) // HEAD
    col = lax.broadcasted_iota(jnp.int32, (width, width), 1) // HEAD
    return jnp.where(row == col, 1.0, 0.0).astype(bf16)


def head_means(values, ones):
    return dot_nn(values.astype(bf16), ones) * (1.0 / HEAD)


def stacked(block):
    first = lax.broadcasted_iota(jnp.int32, block.shape, 1) < HEAD
    zero = jnp.zeros((), block.dtype)
    return jnp.concatenate((jnp.where(first, block, zero), jnp.where(first, zero, block)), axis=0)


def unstacked(block):
    span = block.shape[0] // 2
    first = lax.broadcasted_iota(jnp.int32, (span, block.shape[1]), 1) < HEAD
    return jnp.where(first, block[:span], block[span:])


def attention(q_half, k_half, v_half, grad_att, same_row):
    k_two, v_two = stacked(k_half), stacked(v_half)
    exps = jnp.where(same_row, jnp.exp(dot_nt(q_half, k_two) * gain), 0.0)
    grad_probs = dot_nt(grad_att, v_two)
    probs, d_scores = [], []
    for half in (slice(0, SPAN), slice(SPAN, 2 * SPAN)):
        part = exps[:, half] * (1.0 / jnp.sum(exps[:, half], axis=1, keepdims=True))
        weighted = part * grad_probs[:, half]
        total = jnp.sum(weighted, axis=1, keepdims=True)
        probs.append(part.astype(bf16))
        d_scores.append(((weighted - part * total) * gain).astype(bf16))
    probs, d_scores = jnp.concatenate(probs, axis=1), jnp.concatenate(d_scores, axis=1)
    return (
        dot_nn(probs, v_two).astype(bf16),
        dot_nn(d_scores, k_two),
        unstacked(dot_tn(d_scores, q_half)),
        unstacked(dot_tn(probs, grad_att)).astype(bf16),
    )


def layer_kernel(
    place_ref, counts_ref, rows_ref, up_ref, mine_ref, theirs_ref,
    d_mine_ref, d_theirs_ref, out_mine_ref, out_theirs_ref,
    normed_ref, masked_ref, att_ref,
):
    step = pl.program_id(0)
    tokens = rows_ref.shape[0]
    depth = rows_ref.shape[1]
    width = depth // 2
    own = pl.multiple_of(place_ref[0] * width, width)
    other = pl.multiple_of(width - own, width)
    here = pl.ds(pl.multiple_of(step * tokens, tokens), tokens)
    ones = head_ones(width)

    rows = rows_ref[...].astype(f32)
    inv_rms = lax.rsqrt(jnp.mean(rows * rows, axis=1, keepdims=True) + tiny_eps)
    normed = (rows * inv_rms).astype(bf16)
    normed_ref[here, :] = normed
    slot = lax.broadcasted_iota(jnp.int32, up_ref.shape, 0) // ROW
    masked_ref[here, :] = jnp.where(slot < counts_ref[step], up_ref[...], jnp.zeros((), bf16))

    row_of = lax.broadcasted_iota(jnp.int32, (SPAN, 2 * SPAN), 0) // ROW
    col_of = lax.broadcasted_iota(jnp.int32, (SPAN, 2 * SPAN), 1) % SPAN // ROW
    same_row = row_of == col_of

    for weight_ref, d_ref, heads, place in (
        (theirs_ref, d_theirs_ref, other, 1),
        (mine_ref, d_mine_ref, own, 0),
    ):
        query_key = dot_nn(normed, weight_ref[:depth])
        query, key = query_key[:, :width], query_key[:, width:]
        q_scale = lax.rsqrt(head_means(query * query, ones) + tiny_eps)
        k_scale = lax.rsqrt(head_means(key * key, ones) + tiny_eps)
        q_unit, k_unit = query * q_scale, key * k_scale
        q_half, k_half = q_unit.astype(bf16), k_unit.astype(bf16)
        v_half = dot_nn(normed, weight_ref[depth:, :width]).astype(bf16)
        grad_att = (
            dot_nt(masked_ref[here, pl.ds(own, width)], mine_ref[pl.ds(depth + heads, width), width:])
            + dot_nt(
                masked_ref[here, pl.ds(other, width)], theirs_ref[pl.ds(depth + heads, width), width:]
            )
        ).astype(bf16)
        spans = []
        for low in range(0, tokens, SPAN):
            pairs = []
            for left in range(0, width, 2 * HEAD):
                at = (slice(low, low + SPAN), slice(left, left + 2 * HEAD))
                pairs.append(
                    attention(q_half[at], k_half[at], v_half[at], grad_att[at], same_row)
                )
            spans.append([jnp.concatenate(part, axis=1) for part in zip(*pairs)])
        attended, d_query, d_key, d_value = (
            jnp.concatenate(part, axis=0) for part in zip(*spans)
        )
        att_ref[here, place * width : (place + 1) * width] = attended
        d_ref[here, :width] = (
            q_scale * (d_query - q_unit * head_means(q_unit * d_query, ones))
        ).astype(bf16)
        d_ref[here, width : 2 * width] = (
            k_scale * (d_key - k_unit * head_means(k_unit * d_key, ones))
        ).astype(bf16)
        d_ref[here, 2 * width :] = d_value

    @pl.when(step == pl.num_programs(0) - 1)
    def _():
        for d_ref, out_ref, cols in (
            (d_theirs_ref, out_theirs_ref, other),
            (d_mine_ref, out_mine_ref, own),
        ):
            terms = dot_tn(normed_ref[...], d_ref[...]).astype(bf16)
            out_ref[:depth, :] = terms[:, :depth]
            out_ref[depth:, :width] = terms[:, depth:]
            grads = masked_ref[:, pl.ds(cols, width)]
            for heads, place in ((own, 0), (other, 1)):
                part = att_ref[:, place * width : (place + 1) * width]
                out_ref[pl.ds(depth + heads, width), width:] = dot_tn(part, grads).astype(bf16)


def layer(place, counts, rows, up, mine, theirs):
    tokens, depth = rows.shape
    views = counts.shape[0]
    width = depth // 2
    smem = pl.BlockSpec(memory_space=pltpu.SMEM)
    part = pl.BlockSpec((tokens // views, depth), lambda i: (i, 0))

    def whole(shape):
        return pl.BlockSpec(shape, lambda i: (0, 0))

    outs = [(tokens, 3 * width)] * 2 + [(2 * depth, depth)] * 2
    return pl.pallas_call(
        layer_kernel,
        grid=(views,),
        in_specs=[smem, smem, part, part, whole(mine.shape), whole(theirs.shape)],
        out_specs=[whole(shape) for shape in outs],
        out_shape=[jax.ShapeDtypeStruct(shape, bf16) for shape in outs],
        scratch_shapes=[pltpu.VMEM((tokens, depth), bf16)] * 3,
        compiler_params=pltpu.CompilerParams(vmem_limit_bytes=40 * 1024 * 1024),
        cost_estimate=pl.CostEstimate(
            flops=20 * tokens * depth * depth, bytes_accessed=6 << 20, transcendentals=0
        ),
        name="attention_layer",
    )(place, counts, rows, up, mine, theirs)


MESH_AXES = ("yh", "yl", "core", "x", "z")
ALL_Y = ("yh", "yl")
NEAR = ("yl", "x")


def swapped(block):
    return lax.ppermute(block, "core", [(0, 1), (1, 0)])


def sent(blocks, axis):
    return lax.all_to_all(blocks, axis, split_axis=0, concat_axis=0, tiled=True)


def blocks_of(terms, count):
    return terms.reshape(count, terms.shape[0] // count, terms.shape[1])


def copies_kernel(place_ref, *refs):
    *weight_refs, out_ref = refs
    width = weight_refs[0].shape[1] // 2
    own = pl.multiple_of(place_ref[0] * width, width)
    for yl in range(2):

        @pl.when(place_ref[1] == yl)
        def _():
            for index, weight_ref in enumerate(weight_refs[2 * yl : 2 * yl + 2]):
                block = weight_ref[:, pl.ds(own, width)]
                out_ref[:, :, index * width : (index + 1) * width] = jnp.broadcast_to(
                    block[None], (out_ref.shape[0],) + block.shape
                )


def weight_copies(place, weights, count):
    vmem = pl.BlockSpec(memory_space=pltpu.VMEM)
    return pl.pallas_call(
        copies_kernel,
        in_specs=[pl.BlockSpec(memory_space=pltpu.SMEM)] + [vmem] * 4,
        out_specs=vmem,
        out_shape=jax.ShapeDtypeStruct((count,) + weights[0].shape, bf16),
        name="weight_copies",
    )(place, *weights)


def sum_kernel(blocks_ref, out_ref):
    total = jnp.sum(blocks_ref[...].astype(f32), axis=0).astype(bf16)
    out_ref[...] = jnp.broadcast_to(total, out_ref.shape)


def block_sum(blocks, parts, copies=None):
    count, rows, width = blocks.shape
    out = (rows // parts, width) if copies is None else (copies, rows // parts, width)
    lead = (0,) * (len(out) - 2)
    return pl.pallas_call(
        sum_kernel,
        grid=(parts,),
        in_specs=[pl.BlockSpec((count, rows // parts, width), lambda i: (0, i, 0))],
        out_specs=pl.BlockSpec(out, lambda i: lead + (i, 0)),
        out_shape=jax.ShapeDtypeStruct(out[:-2] + (rows, width), bf16),
        name="block_sum",
    )(blocks)


def final_kernel(scale, blocks_ref, *out_refs):
    count, _, width = blocks_ref.shape
    half = width // 2
    for yl in range(2):
        for core in range(2):
            total = blocks_ref[2 * yl + core].astype(f32)
            for yh in range(1, count // 4):
                total = total + blocks_ref[4 * yh + 2 * yl + core].astype(f32)
            total = total * scale
            cols = slice(core * half, (core + 1) * half)
            out_refs[2 * yl][:, cols] = total[:, :half]
            out_refs[2 * yl + 1][:, cols] = total[:, half:]


def final_sum(blocks, scale):
    _, rows, width = blocks.shape
    vmem = pl.BlockSpec(memory_space=pltpu.VMEM)
    return pl.pallas_call(
        functools.partial(final_kernel, scale),
        in_specs=[vmem],
        out_specs=[vmem] * 4,
        out_shape=[jax.ShapeDtypeStruct((rows, width), f32)] * 4,
        name="final_sum",
    )(blocks)


def local(trace_rows, upstream, counts, w_query, w_key, w_value, w_out):
    place = jnp.stack((lax.axis_index("core"), lax.axis_index("yl")))
    view_count, most_rows, row_length, depth = trace_rows.shape
    tokens = view_count * most_rows * row_length
    view_counts = counts.reshape(view_count)

    copies = weight_copies(place, (w_query, w_key, w_value, w_out), lax.axis_size("z"))
    lines = sent(copies, "z").reshape(-1, depth)
    lines = jnp.broadcast_to(lines[None], (lax.axis_size(NEAR),) + lines.shape)
    mine = sent(lines, NEAR).reshape(-1, depth)
    theirs = swapped(mine)

    rows, up = trace_rows.reshape(tokens, depth), upstream.reshape(tokens, depth)
    d_mine, d_theirs, out_mine, out_theirs = layer(place, view_counts, rows, up, mine, theirs)

    terms = (out_mine.astype(f32) + swapped(out_theirs).astype(f32)).astype(bf16)
    total = block_sum(sent(blocks_of(terms, lax.axis_size(NEAR)), NEAR), 4)
    total = sent(blocks_of(total, lax.axis_size("z")), "z")
    total = block_sum(total, 1, lax.axis_size(ALL_Y + ("core",)))
    devices = math.prod(lax.axis_size(name) for name in MESH_AXES)
    weight_grads = final_sum(
        sent(total, ALL_Y + ("core",)), 1.0 / math.sqrt(devices * tokens // 2)
    )

    grad_norm = sum(
        dot_nt(d[:, :depth], weights[:depth])
        + dot_nt(d[:, depth:], weights[depth:, : depth // 2])
        for d, weights in ((d_mine, mine), (d_theirs, theirs))
    )
    rows = rows.astype(f32)
    inv_rms = lax.rsqrt(jnp.mean(rows * rows, axis=-1, keepdims=True) + tiny_eps)
    scaled = rows * inv_rms
    is_live = lax.iota(jnp.int32, most_rows)[None, :] < view_counts[:, None]
    is_live = jnp.repeat(is_live.reshape(-1), row_length)[:, None]
    masked = jnp.where(is_live, up, jnp.zeros((), up.dtype)).astype(f32)
    done = masked + inv_rms * (
        grad_norm - scaled * jnp.mean(scaled * grad_norm, axis=-1, keepdims=True)
    )
    return (done.astype(bf16).reshape(trace_rows.shape), *weight_grads)


def solution(mesh):
    fine_mesh = jax.sharding.Mesh(mesh.devices.reshape(4, 2, 2, 4, 8), MESH_AXES)
    every, peer = P(MESH_AXES), P(("x", "z"), None)
    in_specs = (every, every, P(("yh", "yl", "core"), ("x", "z")), peer, peer, peer, peer)
    out_specs = (every, peer, peer, peer, peer)
    return jax.shard_map(
        local, mesh=fine_mesh, in_specs=in_specs, out_specs=out_specs, check_vma=False
    )
```

```python
import functools
import math
import jax
import jax.numpy as jnp
from jax import lax
from jax.experimental import pallas as pl
from jax.experimental.pallas import tpu as pltpu
from jax.sharding import PartitionSpec as P

HEAD = 64
ROW = 32
SPAN = 128
gain = 6.0 / HEAD
tiny_eps = 1e-06
f32, bf16 = jnp.float32, jnp.bfloat16


def dot_nn(a, b):
    return lax.dot_general(a, b, (((1,), (0,)), ((), ())), preferred_element_type=f32)


def dot_nt(a, b):
    return lax.dot_general(a, b, (((1,), (1,)), ((), ())), preferred_element_type=f32)


def dot_tn(a, b):
    return lax.dot_general(a, b, (((0,), (0,)), ((), ())), preferred_element_type=f32)


def head_ones(width):
    row = lax.broadcasted_iota(jnp.int32, (width, width), 0) // HEAD
    col = lax.broadcasted_iota(jnp.int32, (width, width), 1) // HEAD
    return jnp.where(row == col, 1.0, 0.0).astype(bf16)


def head_means(values, ones):
    return dot_nn(values.astype(bf16), ones) * (1.0 / HEAD)


def stacked(block):
    first = lax.broadcasted_iota(jnp.int32, block.shape, 1) < HEAD
    zero = jnp.zeros((), block.dtype)
    return jnp.concatenate((jnp.where(first, block, zero), jnp.where(first, zero, block)), axis=0)


def unstacked(block):
    span = block.shape[0] // 2
    first = lax.broadcasted_iota(jnp.int32, (span, block.shape[1]), 1) < HEAD
    return jnp.where(first, block[:span], block[span:])


def attention(q_half, k_half, v_half, grad_att, same_row):
    k_two, v_two = stacked(k_half), stacked(v_half)
    exps = jnp.where(same_row, jnp.exp(dot_nt(k_two, q_half) * gain), 0.0)
    grad_probs = dot_nt(v_two, grad_att)
    probs, d_scores = [], []
    for half in (slice(0, SPAN), slice(SPAN, 2 * SPAN)):
        part = exps[half] * (1.0 / jnp.sum(exps[half], axis=0, keepdims=True))
        weighted = part * grad_probs[half]
        total = jnp.sum(weighted, axis=0, keepdims=True)
        probs.append(part.astype(bf16))
        d_scores.append(((weighted - part * total) * gain).astype(bf16))
    probs, d_scores = jnp.concatenate(probs, axis=0), jnp.concatenate(d_scores, axis=0)
    return (
        dot_tn(probs, v_two).astype(bf16),
        dot_tn(d_scores, k_two),
        unstacked(dot_nn(d_scores, q_half)),
        unstacked(dot_nn(probs, grad_att)).astype(bf16),
    )


def layer_kernel(
    place_ref, counts_ref, rows_ref, up_ref, mine_ref, theirs_ref,
    d_mine_ref, d_theirs_ref, out_mine_ref, out_theirs_ref,
    normed_ref, masked_ref, att_ref,
):
    step = pl.program_id(0)
    tokens = rows_ref.shape[0]
    depth = rows_ref.shape[1]
    width = depth // 2
    own = pl.multiple_of(place_ref[0] * width, width)
    other = pl.multiple_of(width - own, width)
    here = pl.ds(pl.multiple_of(step * tokens, tokens), tokens)
    ones = head_ones(width)

    rows = rows_ref[...].astype(f32)
    inv_rms = lax.rsqrt(jnp.mean(rows * rows, axis=1, keepdims=True) + tiny_eps)
    normed = (rows * inv_rms).astype(bf16)
    normed_ref[here, :] = normed
    slot = lax.broadcasted_iota(jnp.int32, up_ref.shape, 0) // ROW
    masked_ref[here, :] = jnp.where(slot < counts_ref[step], up_ref[...], jnp.zeros((), bf16))

    row_of = lax.broadcasted_iota(jnp.int32, (2 * SPAN, SPAN), 0) % SPAN // ROW
    col_of = lax.broadcasted_iota(jnp.int32, (2 * SPAN, SPAN), 1) // ROW
    same_row = row_of == col_of

    for weight_ref, d_ref, heads, place in (
        (theirs_ref, d_theirs_ref, other, 1),
        (mine_ref, d_mine_ref, own, 0),
    ):
        query_key = dot_nn(normed, weight_ref[:depth])
        query, key = query_key[:, :width], query_key[:, width:]
        q_scale = lax.rsqrt(head_means(query * query, ones) + tiny_eps)
        k_scale = lax.rsqrt(head_means(key * key, ones) + tiny_eps)
        q_unit, k_unit = query * q_scale, key * k_scale
        q_half, k_half = q_unit.astype(bf16), k_unit.astype(bf16)
        v_half = dot_nn(normed, weight_ref[depth:, :width]).astype(bf16)
        grad_att = (
            dot_nt(masked_ref[here, pl.ds(own, width)], mine_ref[pl.ds(depth + heads, width), width:])
            + dot_nt(
                masked_ref[here, pl.ds(other, width)], theirs_ref[pl.ds(depth + heads, width), width:]
            )
        ).astype(bf16)
        spans = []
        for low in range(0, tokens, SPAN):
            pairs = []
            for left in range(0, width, 2 * HEAD):
                at = (slice(low, low + SPAN), slice(left, left + 2 * HEAD))
                pairs.append(
                    attention(q_half[at], k_half[at], v_half[at], grad_att[at], same_row)
                )
            spans.append([jnp.concatenate(part, axis=1) for part in zip(*pairs)])
        attended, d_query, d_key, d_value = (
            jnp.concatenate(part, axis=0) for part in zip(*spans)
        )
        att_ref[here, place * width : (place + 1) * width] = attended
        d_ref[here, :width] = (
            q_scale * (d_query - q_unit * head_means(q_unit * d_query, ones))
        ).astype(bf16)
        d_ref[here, width : 2 * width] = (
            k_scale * (d_key - k_unit * head_means(k_unit * d_key, ones))
        ).astype(bf16)
        d_ref[here, 2 * width :] = d_value

    @pl.when(step == pl.num_programs(0) - 1)
    def _():
        for d_ref, out_ref, cols in (
            (d_theirs_ref, out_theirs_ref, other),
            (d_mine_ref, out_mine_ref, own),
        ):
            terms = dot_tn(normed_ref[...], d_ref[...]).astype(bf16)
            out_ref[:depth, :] = terms[:, :depth]
            out_ref[depth:, :width] = terms[:, depth:]
            grads = masked_ref[:, pl.ds(cols, width)]
            for heads, place in ((own, 0), (other, 1)):
                part = att_ref[:, place * width : (place + 1) * width]
                out_ref[pl.ds(depth + heads, width), width:] = dot_tn(part, grads).astype(bf16)


def layer(place, counts, rows, up, mine, theirs):
    tokens, depth = rows.shape
    views = counts.shape[0]
    width = depth // 2
    smem = pl.BlockSpec(memory_space=pltpu.SMEM)
    part = pl.BlockSpec((tokens // views, depth), lambda i: (i, 0))

    def whole(shape):
        return pl.BlockSpec(shape, lambda i: (0, 0))

    outs = [(tokens, 3 * width)] * 2 + [(2 * depth, depth)] * 2
    return pl.pallas_call(
        layer_kernel,
        grid=(views,),
        in_specs=[smem, smem, part, part, whole(mine.shape), whole(theirs.shape)],
        out_specs=[whole(shape) for shape in outs],
        out_shape=[jax.ShapeDtypeStruct(shape, bf16) for shape in outs],
        scratch_shapes=[pltpu.VMEM((tokens, depth), bf16)] * 3,
        compiler_params=pltpu.CompilerParams(vmem_limit_bytes=40 * 1024 * 1024),
        cost_estimate=pl.CostEstimate(
            flops=20 * tokens * depth * depth, bytes_accessed=6 << 20, transcendentals=0
        ),
        name="attention_layer",
    )(place, counts, rows, up, mine, theirs)


MESH_AXES = ("yh", "yl", "core", "x", "z")
ALL_Y = ("yh", "yl")
NEAR = ("yl", "x")


def swapped(block):
    return lax.ppermute(block, "core", [(0, 1), (1, 0)])


def sent(blocks, axis):
    return lax.all_to_all(blocks, axis, split_axis=0, concat_axis=0, tiled=True)


def blocks_of(terms, count):
    return terms.reshape(count, terms.shape[0] // count, terms.shape[1])


def weight_copies(core, yl, weights, count):
    width = weights[0].shape[1] // 2
    halves = [jnp.where(core == 0, weight[:, :width], weight[:, width:]) for weight in weights]
    block = jnp.concatenate(
        [jnp.where(yl == 0, halves[index], halves[index + 2]) for index in range(2)], axis=1
    )
    return jnp.broadcast_to(block[None], (count,) + block.shape)


small = pltpu.CompilerParams(vmem_limit_bytes=4 * 1024 * 1024)


def sum_kernel(blocks_ref, out_ref):
    out_ref[...] = jnp.sum(blocks_ref[...].astype(f32), axis=0).astype(bf16)


def block_sum(blocks):
    vmem = pl.BlockSpec(memory_space=pltpu.VMEM)
    return pl.pallas_call(
        sum_kernel,
        in_specs=[vmem],
        out_specs=vmem,
        out_shape=jax.ShapeDtypeStruct(blocks.shape[1:], bf16),
        compiler_params=small,
        name="block_sum",
    )(blocks)


def final_kernel(scale, blocks_ref, *out_refs):
    count, _, width = blocks_ref.shape
    half = width // 2
    for yl in range(2):
        for core in range(2):
            total = blocks_ref[2 * yl + core].astype(f32)
            for yh in range(1, count // 4):
                total = total + blocks_ref[4 * yh + 2 * yl + core].astype(f32)
            total = total * scale
            cols = slice(core * half, (core + 1) * half)
            out_refs[2 * yl][:, cols] = total[:, :half]
            out_refs[2 * yl + 1][:, cols] = total[:, half:]


def final_sum(blocks, scale):
    _, rows, width = blocks.shape
    vmem = pl.BlockSpec(memory_space=pltpu.VMEM)
    return pl.pallas_call(
        functools.partial(final_kernel, scale),
        in_specs=[vmem],
        out_specs=[vmem] * 4,
        out_shape=[jax.ShapeDtypeStruct((rows, width), f32)] * 4,
        compiler_params=small,
        name="final_sum",
    )(blocks)


def local(trace_rows, upstream, counts, w_query, w_key, w_value, w_out):
    core, yl = lax.axis_index("core"), lax.axis_index("yl")
    view_count, most_rows, row_length, depth = trace_rows.shape
    tokens = view_count * most_rows * row_length
    view_counts = counts.reshape(view_count)

    copies = weight_copies(core, yl, (w_query, w_key, w_value, w_out), lax.axis_size("z"))
    lines = sent(copies, "z").reshape(-1, depth)
    lines = jnp.broadcast_to(lines[None], (lax.axis_size(NEAR),) + lines.shape)
    mine = sent(lines, NEAR).reshape(-1, depth)
    theirs = swapped(mine)

    rows, up = trace_rows.reshape(tokens, depth), upstream.reshape(tokens, depth)
    d_mine, d_theirs, out_mine, out_theirs = layer(core.reshape(1), view_counts, rows, up, mine, theirs)

    terms = (out_mine.astype(f32) + swapped(out_theirs).astype(f32)).astype(bf16)
    total = block_sum(sent(blocks_of(terms, lax.axis_size(NEAR)), NEAR))
    total = sent(blocks_of(total, lax.axis_size("z")), "z")
    total = jnp.sum(total.astype(f32), axis=0).astype(bf16)
    total = jnp.broadcast_to(total[None], (lax.axis_size(ALL_Y + ("core",)),) + total.shape)
    devices = math.prod(lax.axis_size(name) for name in MESH_AXES)
    weight_grads = final_sum(
        sent(total, ALL_Y + ("core",)), 1.0 / math.sqrt(devices * tokens // 2)
    )

    grad_norm = sum(
        dot_nt(d[:, :depth], weights[:depth])
        + dot_nt(d[:, depth:], weights[depth:, : depth // 2])
        for d, weights in ((d_mine, mine), (d_theirs, theirs))
    )
    rows = rows.astype(f32)
    inv_rms = lax.rsqrt(jnp.mean(rows * rows, axis=-1, keepdims=True) + tiny_eps)
    scaled = rows * inv_rms
    is_live = lax.iota(jnp.int32, most_rows)[None, :] < view_counts[:, None]
    is_live = jnp.repeat(is_live.reshape(-1), row_length)[:, None]
    masked = jnp.where(is_live, up, jnp.zeros((), up.dtype)).astype(f32)
    done = masked + inv_rms * (
        grad_norm - scaled * jnp.mean(scaled * grad_norm, axis=-1, keepdims=True)
    )
    return (done.astype(bf16).reshape(trace_rows.shape), *weight_grads)


def solution(mesh):
    fine_mesh = jax.sharding.Mesh(mesh.devices.reshape(4, 2, 2, 4, 8), MESH_AXES)
    every, peer = P(MESH_AXES), P(("x", "z"), None)
    in_specs = (every, every, P(("yh", "yl", "core"), ("x", "z")), peer, peer, peer, peer)
    out_specs = (every, peer, peer, peer, peer)
    return jax.shard_map(
        local, mesh=fine_mesh, in_specs=in_specs, out_specs=out_specs, check_vma=False
    )
```

```python
import functools
import math
import jax
import jax.numpy as jnp
from jax import lax
from jax.experimental import pallas as pl
from jax.experimental.pallas import tpu as pltpu
from jax.sharding import PartitionSpec as P

HEAD = 64
ROW = 32
SPAN = 128
STEP = 256
gain = 6.0 / HEAD
tiny_eps = 1e-06
f32, bf16 = jnp.float32, jnp.bfloat16


def dot_nn(a, b):
    return lax.dot_general(a, b, (((1,), (0,)), ((), ())), preferred_element_type=f32)


def dot_nt(a, b):
    return lax.dot_general(a, b, (((1,), (1,)), ((), ())), preferred_element_type=f32)


def dot_tn(a, b):
    return lax.dot_general(a, b, (((0,), (0,)), ((), ())), preferred_element_type=f32)


def head_ones(width):
    row = lax.broadcasted_iota(jnp.int32, (width, width), 0) // HEAD
    col = lax.broadcasted_iota(jnp.int32, (width, width), 1) // HEAD
    return jnp.where(row == col, 1.0, 0.0).astype(bf16)


def head_means(values, ones):
    return dot_nn(values.astype(bf16), ones) * (1.0 / HEAD)


def stacked(block):
    first = lax.broadcasted_iota(jnp.int32, block.shape, 1) < HEAD
    zero = jnp.zeros((), block.dtype)
    return jnp.concatenate((jnp.where(first, block, zero), jnp.where(first, zero, block)), axis=0)


def unstacked(block):
    span = block.shape[0] // 2
    first = lax.broadcasted_iota(jnp.int32, (span, block.shape[1]), 1) < HEAD
    return jnp.where(first, block[:span], block[span:])


def attention(q_half, k_half, v_half, grad_att, same_row):
    k_two, v_two = stacked(k_half), stacked(v_half)
    exps = jnp.where(same_row, jnp.exp(dot_nt(k_two, q_half) * gain), 0.0)
    grad_probs = dot_nt(v_two, grad_att)
    probs, d_scores = [], []
    for half in (slice(0, SPAN), slice(SPAN, 2 * SPAN)):
        part = exps[half] * (1.0 / jnp.sum(exps[half], axis=0, keepdims=True))
        weighted = part * grad_probs[half]
        total = jnp.sum(weighted, axis=0, keepdims=True)
        probs.append(part.astype(bf16))
        d_scores.append(((weighted - part * total) * gain).astype(bf16))
    probs, d_scores = jnp.concatenate(probs, axis=0), jnp.concatenate(d_scores, axis=0)
    return (
        dot_tn(probs, v_two).astype(bf16),
        dot_tn(d_scores, k_two),
        unstacked(dot_nn(d_scores, q_half)),
        unstacked(dot_nn(probs, grad_att)).astype(bf16),
    )


def layer_kernel(
    rows_a_ref, rows_b_ref, grads_a_ref, grads_b_ref, weights_ref,
    d_ref, out_ref, normed_ref, grads_ref, att_ref, wo_ref,
):
    step = pl.program_id(0)
    held, depth = rows_a_ref.shape
    width = depth // 2
    here = pl.ds(pl.multiple_of(step * STEP, STEP), STEP)

    @pl.when(step == 0)
    def _():
        for low, rows_ref, part_ref in (
            (0, rows_a_ref, grads_a_ref),
            (held, rows_b_ref, grads_b_ref),
        ):
            rows = rows_ref[...].astype(f32)
            inv_rms = lax.rsqrt(jnp.mean(rows * rows, axis=1, keepdims=True) + tiny_eps)
            normed_ref[low : low + held, :] = (rows * inv_rms).astype(bf16)
            grads_ref[low : low + held, :] = part_ref[...]
        for low in range(0, width, HEAD):
            for half in range(2):
                at = depth + 2 * low + half * HEAD
                wo_ref[low : low + HEAD, half * width : (half + 1) * width] = weights_ref[
                    at : at + HEAD, width:
                ]

    ones = head_ones(width)
    normed = normed_ref[here, :]
    row_of = lax.broadcasted_iota(jnp.int32, (2 * SPAN, SPAN), 0) % SPAN // ROW
    col_of = lax.broadcasted_iota(jnp.int32, (2 * SPAN, SPAN), 1) // ROW
    same_row = row_of == col_of

    query_key = dot_nn(normed, weights_ref[:depth])
    query, key = query_key[:, :width], query_key[:, width:]
    q_scale = lax.rsqrt(head_means(query * query, ones) + tiny_eps)
    k_scale = lax.rsqrt(head_means(key * key, ones) + tiny_eps)
    q_unit, k_unit = query * q_scale, key * k_scale
    q_half, k_half = q_unit.astype(bf16), k_unit.astype(bf16)
    v_half = dot_nn(normed, weights_ref[depth:, :width]).astype(bf16)
    grad_att = dot_nt(grads_ref[here, :], wo_ref[...]).astype(bf16)
    spans = []
    for low in range(0, STEP, SPAN):
        pairs = []
        for left in range(0, width, 2 * HEAD):
            at = (slice(low, low + SPAN), slice(left, left + 2 * HEAD))
            pairs.append(attention(q_half[at], k_half[at], v_half[at], grad_att[at], same_row))
        spans.append([jnp.concatenate(part, axis=1) for part in zip(*pairs)])
    attended, d_query, d_key, d_value = (jnp.concatenate(part, axis=0) for part in zip(*spans))
    att_ref[here, :] = attended
    d_ref[here, :width] = (
        q_scale * (d_query - q_unit * head_means(q_unit * d_query, ones))
    ).astype(bf16)
    d_ref[here, width:depth] = (
        k_scale * (d_key - k_unit * head_means(k_unit * d_key, ones))
    ).astype(bf16)
    d_ref[here, depth:] = d_value

    @pl.when(step == pl.num_programs(0) - 1)
    def _():
        terms = dot_tn(normed_ref[...], d_ref[...]).astype(bf16)
        out_ref[:depth, :] = terms[:, :depth]
        out_ref[depth:, :width] = terms[:, depth:]
        out_terms = dot_tn(att_ref[...], grads_ref[...]).astype(bf16)
        for low in range(0, width, HEAD):
            for half in range(2):
                at = depth + 2 * low + half * HEAD
                out_ref[at : at + HEAD, width:] = out_terms[
                    low : low + HEAD, half * width : (half + 1) * width
                ]


def layer(rows_a, rows_b, grads_a, grads_b, weights):
    held, depth = rows_a.shape
    tokens = 2 * held

    def whole(shape):
        return pl.BlockSpec(shape, lambda i: (0, 0))

    outs = [(tokens, 3 * depth // 2), weights.shape]
    ins = (rows_a, rows_b, grads_a, grads_b, weights)
    return pl.pallas_call(
        layer_kernel,
        grid=(tokens // STEP,),
        in_specs=[whole(array.shape) for array in ins],
        out_specs=[whole(shape) for shape in outs],
        out_shape=[jax.ShapeDtypeStruct(shape, bf16) for shape in outs],
        scratch_shapes=[
            pltpu.VMEM((tokens, depth), bf16),
            pltpu.VMEM((tokens, depth), bf16),
            pltpu.VMEM((tokens, depth // 2), bf16),
            pltpu.VMEM((depth // 2, depth), bf16),
        ],
        compiler_params=pltpu.CompilerParams(vmem_limit_bytes=40 * 1024 * 1024),
        cost_estimate=pl.CostEstimate(
            flops=10 * tokens * depth * depth, bytes_accessed=6 << 20, transcendentals=0
        ),
        name="attention_layer",
    )(*ins)


MESH_AXES = ("yh", "yl", "core", "x", "z")
ALL_Y = ("yh", "yl")
NEAR = ("yl", "x")


def swapped(block):
    return lax.ppermute(block, "core", [(0, 1), (1, 0)])


def sent(blocks, axis):
    return lax.all_to_all(blocks, axis, split_axis=0, concat_axis=0, tiled=True)


def blocks_of(terms, count):
    return terms.reshape(count, terms.shape[0] // count, terms.shape[1])


small = pltpu.CompilerParams(vmem_limit_bytes=8 * 1024 * 1024)


def head_lanes(shape):
    return lax.broadcasted_iota(jnp.int32, shape, 1) < HEAD


def core_heads(tiles, core):
    packed = []
    for low, high in zip(tiles[::2], tiles[1::2]):
        first = head_lanes(low.shape)
        moved = jnp.where(core == 0, high, low)
        kept = jnp.where(core == 0, low, high)
        moved = pltpu.roll(moved, HEAD, 1)
        packed.append(jnp.where(first == (core == 0), kept, moved))
    return jnp.concatenate(packed, axis=1)


def tiles_of(block):
    return [block[:, low : low + 2 * HEAD] for low in range(0, block.shape[1], 2 * HEAD)]


def copies_kernel(core_ref, yl_ref, wq_ref, wk_ref, wv_ref, wo_ref, out_ref):
    core, yl = core_ref[0], yl_ref[0]
    half = wq_ref.shape[1] // 2

    def write(parts):
        low = 0
        for part in parts:
            out_ref[:, :, low : low + part.shape[1]] = jnp.broadcast_to(
                part.astype(bf16)[None], (out_ref.shape[0],) + part.shape
            )
            low += part.shape[1]

    def own(weight_ref):
        return core_heads(tiles_of(weight_ref[...].astype(f32)), core)

    @pl.when(yl == 0)
    def _():
        write((own(wq_ref), own(wk_ref), wo_ref[:, :half]))

    @pl.when(yl == 1)
    def _():
        write((own(wv_ref), wo_ref[...]))


def weight_copies(core, yl, weights, count):
    rows, width = weights[0].shape
    smem, vmem = (pl.BlockSpec(memory_space=space) for space in (pltpu.SMEM, pltpu.VMEM))
    return pl.pallas_call(
        copies_kernel,
        in_specs=[smem, smem] + [vmem] * 4,
        out_specs=vmem,
        out_shape=jax.ShapeDtypeStruct((count, rows, 3 * width // 2), bf16),
        compiler_params=small,
        name="weight_copies",
    )(core, yl, *weights)


def lines_kernel(core_ref, yl_ref, blocks_ref, out_ref):
    count, rows, width = blocks_ref.shape
    depth, half = 2 * width // 3, width // 3
    near = out_ref.shape[0]

    def write(low, part):
        out_ref[:, :, low : low + part.shape[1]] = jnp.broadcast_to(
            part[None], (near,) + part.shape
        )

    @pl.when(yl_ref[0] == 0)
    def _():
        write(0, blocks_ref[:, :, :depth].reshape(count * rows, depth))

    @pl.when(yl_ref[0] == 1)
    def _():
        write(0, blocks_ref[:, :, :half].reshape(count * rows, half))
        heads = blocks_ref[pl.ds(core_ref[0] * (count // 2), count // 2), :, half:]
        heads = heads.reshape(count // 2 * rows, depth)
        write(half, jnp.concatenate((heads[:, :half], heads[:, half:]), axis=0))


def weight_lines(core, yl, blocks, copies):
    count, rows, width = blocks.shape
    smem, vmem = (pl.BlockSpec(memory_space=space) for space in (pltpu.SMEM, pltpu.VMEM))
    return pl.pallas_call(
        lines_kernel,
        in_specs=[smem, smem, vmem],
        out_specs=vmem,
        out_shape=jax.ShapeDtypeStruct((copies, count * rows, 2 * width // 3), bf16),
        compiler_params=small,
        name="weight_lines",
    )(core, yl, blocks)


def near_sum_kernel(core_ref, yl_ref, blocks_ref, out_ref):
    total = jnp.sum(blocks_ref[...].astype(f32), axis=0).astype(bf16)
    count, rows, _ = out_ref.shape
    depth = total.shape[1]
    half = depth // 2

    @pl.when(yl_ref[0] == 0)
    def _():
        out_ref[:, :, :depth] = total.reshape(count, rows, depth)
        out_ref[:, :, depth:] = jnp.zeros((count, rows, half), bf16)

    @pl.when(yl_ref[0] == 1)
    def _():
        out_ref[:, :, :half] = total[:, :half].reshape(count, rows, half)
        out_ref[:, :, half:] = jnp.zeros((count, rows, depth), bf16)
        here = pl.ds(core_ref[0] * (count // 2), count // 2)
        heads = total[:, half:].reshape(2, count // 2, rows, half)
        out_ref[here, :, half:depth] = heads[0]
        out_ref[here, :, depth:] = heads[1]


def near_sum(core, yl, blocks, count):
    _, rows, depth = blocks.shape
    smem, vmem = (pl.BlockSpec(memory_space=space) for space in (pltpu.SMEM, pltpu.VMEM))
    return pl.pallas_call(
        near_sum_kernel,
        in_specs=[smem, smem, vmem],
        out_specs=vmem,
        out_shape=jax.ShapeDtypeStruct((count, rows // count, 3 * depth // 2), bf16),
        compiler_params=small,
        name="near_sum",
    )(core, yl, blocks)


def final_kernel(scale, blocks_ref, *out_refs):
    count, _, width = blocks_ref.shape
    depth, half = 2 * width // 3, width // 3
    totals = []
    for place in range(4):
        total = blocks_ref[place].astype(f32)
        for yh in range(1, count // 4):
            total = total + blocks_ref[4 * yh + place].astype(f32)
        totals.append(total * scale)
    (first_a, first_b), (second_a, second_b) = totals[:2], totals[2:]
    for out_ref, one, two in (
        (out_refs[0], first_a[:, :half], first_b[:, :half]),
        (out_refs[1], first_a[:, half:depth], first_b[:, half:depth]),
        (out_refs[2], second_a[:, :half], second_b[:, :half]),
    ):
        low = 0
        for tile_one, tile_two in zip(tiles_of(one), tiles_of(two)):
            first = head_lanes(tile_one.shape)
            for place, pair in enumerate(
                ((tile_one, pltpu.roll(tile_two, HEAD, 1)), (pltpu.roll(tile_one, HEAD, 1), tile_two))
            ):
                out_ref[:, low : low + 2 * HEAD] = jnp.where(first, *pair)
                low += 2 * HEAD
    out_refs[3][...] = second_a[:, half:] + second_b[:, half:]


def final_sum(blocks, scale):
    _, rows, width = blocks.shape
    width = 2 * width // 3
    vmem = pl.BlockSpec(memory_space=pltpu.VMEM)
    return pl.pallas_call(
        functools.partial(final_kernel, scale),
        in_specs=[vmem],
        out_specs=[vmem] * 4,
        out_shape=[jax.ShapeDtypeStruct((rows, width), f32)] * 4,
        compiler_params=small,
        name="final_sum",
    )(blocks)


def local(trace_rows, upstream, counts, w_query, w_key, w_value, w_out):
    core, yl = lax.axis_index("core").reshape(1), lax.axis_index("yl").reshape(1)
    view_count, most_rows, row_length, depth = trace_rows.shape
    tokens = view_count * most_rows * row_length
    view_counts = counts.reshape(view_count)

    copies = weight_copies(core, yl, (w_query, w_key, w_value, w_out), lax.axis_size("z"))
    rows, up = trace_rows.reshape(tokens, depth), upstream.reshape(tokens, depth)
    is_live = lax.iota(jnp.int32, most_rows)[None, :] < view_counts[:, None]
    is_live = jnp.repeat(is_live.reshape(-1), row_length)[:, None]
    masked = jnp.where(is_live, up, jnp.zeros((), up.dtype))
    blocks, other_rows, other_masked = lax.optimization_barrier(
        (sent(copies, "z"), swapped(rows), swapped(masked))
    )
    lines = weight_lines(core, yl, blocks, lax.axis_size(NEAR))
    weights = sent(lines, NEAR).reshape(-1, depth)

    d_qkv, terms = layer(rows, other_rows, masked, other_masked, weights)

    z_count = lax.axis_size("z")
    total = near_sum(core, yl, sent(blocks_of(terms, lax.axis_size(NEAR)), NEAR), z_count)
    total = jnp.sum(sent(total, "z").astype(f32), axis=0).astype(bf16)
    total = jnp.broadcast_to(total[None], (lax.axis_size(ALL_Y + ("core",)),) + total.shape)
    devices = math.prod(lax.axis_size(name) for name in MESH_AXES)
    weight_grads = final_sum(
        sent(total, ALL_Y + ("core",)), 1.0 / math.sqrt(devices * tokens // 2)
    )

    grad_norm = dot_nt(d_qkv[:, :depth], weights[:depth]) + dot_nt(
        d_qkv[:, depth:], weights[depth:, : depth // 2]
    )
    grad_norm = grad_norm[:tokens] + swapped(grad_norm[tokens:].astype(bf16)).astype(f32)
    rows = rows.astype(f32)
    inv_rms = lax.rsqrt(jnp.mean(rows * rows, axis=-1, keepdims=True) + tiny_eps)
    scaled = rows * inv_rms
    done = masked.astype(f32) + inv_rms * (
        grad_norm - scaled * jnp.mean(scaled * grad_norm, axis=-1, keepdims=True)
    )
    return (done.astype(bf16).reshape(trace_rows.shape), *weight_grads)


def solution(mesh):
    fine_mesh = jax.sharding.Mesh(mesh.devices.reshape(4, 2, 2, 4, 8), MESH_AXES)
    every, peer = P(MESH_AXES), P(("x", "z"), None)
    in_specs = (every, every, P(("yh", "yl", "core"), ("x", "z")), peer, peer, peer, peer)
    out_specs = (every, peer, peer, peer, peer)
    return jax.shard_map(
        local, mesh=fine_mesh, in_specs=in_specs, out_specs=out_specs, check_vma=False
    )
```

```python
import functools
import math
import jax
import jax.numpy as jnp
from jax import lax
from jax.experimental import pallas as pl
from jax.experimental.pallas import tpu as pltpu
from jax.sharding import PartitionSpec as P

HEAD = 64
ROW = 32
SPAN = 128
STEP = 256
gain = 6.0 / HEAD
tiny_eps = 1e-06
f32, bf16 = jnp.float32, jnp.bfloat16


def dot_nn(a, b):
    return lax.dot_general(a, b, (((1,), (0,)), ((), ())), preferred_element_type=f32)


def dot_nt(a, b):
    return lax.dot_general(a, b, (((1,), (1,)), ((), ())), preferred_element_type=f32)


def dot_tn(a, b):
    return lax.dot_general(a, b, (((0,), (0,)), ((), ())), preferred_element_type=f32)


def head_ones(width):
    row = lax.broadcasted_iota(jnp.int32, (width, width), 0) // HEAD
    col = lax.broadcasted_iota(jnp.int32, (width, width), 1) // HEAD
    return jnp.where(row == col, 1.0, 0.0).astype(bf16)


def head_means(values, ones):
    return dot_nn(values.astype(bf16), ones) * (1.0 / HEAD)


def stacked(block):
    first = lax.broadcasted_iota(jnp.int32, block.shape, 1) < HEAD
    zero = jnp.zeros((), block.dtype)
    return jnp.concatenate((jnp.where(first, block, zero), jnp.where(first, zero, block)), axis=0)


def unstacked(block):
    span = block.shape[0] // 2
    first = lax.broadcasted_iota(jnp.int32, (span, block.shape[1]), 1) < HEAD
    return jnp.where(first, block[:span], block[span:])


def attention(q_half, k_half, v_half, grad_att, same_row):
    k_two, v_two = stacked(k_half), stacked(v_half)
    exps = jnp.where(same_row, jnp.exp(dot_nt(k_two, q_half) * gain), 0.0)
    grad_probs = dot_nt(v_two, grad_att)
    probs, d_scores = [], []
    for half in (slice(0, SPAN), slice(SPAN, 2 * SPAN)):
        part = exps[half] * (1.0 / jnp.sum(exps[half], axis=0, keepdims=True))
        weighted = part * grad_probs[half]
        total = jnp.sum(weighted, axis=0, keepdims=True)
        probs.append(part.astype(bf16))
        d_scores.append(((weighted - part * total) * gain).astype(bf16))
    probs, d_scores = jnp.concatenate(probs, axis=0), jnp.concatenate(d_scores, axis=0)
    return (
        dot_tn(probs, v_two).astype(bf16),
        dot_tn(d_scores, k_two),
        unstacked(dot_nn(d_scores, q_half)),
        unstacked(dot_nn(probs, grad_att)).astype(bf16),
    )


def layer_kernel(
    normed_ref, grads_ref, weights_ref, d_out_ref, terms_ref, d_ref, out_ref, att_ref, wo_ref, sems
):
    step = pl.program_id(0)
    depth = normed_ref.shape[1]
    width, tile = depth // 2, 2 * HEAD
    used = width + tile
    here = pl.ds(pl.multiple_of(step * STEP, STEP), STEP)

    def wo_parts():
        for low in range(0, width, HEAD):
            for part in range(4):
                at = part // 2 * depth + 2 * low + part % 2 * HEAD
                rows, cols = slice(low, low + HEAD), slice(part * tile, (part + 1) * tile)
                yield (rows, cols), (slice(at, at + HEAD), slice(used, depth))

    @pl.when(step == 0)
    def _():
        for inner, outer in wo_parts():
            wo_ref[inner] = weights_ref[outer]

    ones = head_ones(width)
    normed = normed_ref[here, :]
    row_of = lax.broadcasted_iota(jnp.int32, (2 * SPAN, SPAN), 0) % SPAN // ROW
    col_of = lax.broadcasted_iota(jnp.int32, (2 * SPAN, SPAN), 1) // ROW
    same_row = row_of == col_of

    first = dot_nn(normed, weights_ref[:depth, :used])
    second = dot_nn(normed, weights_ref[depth:, :used])
    query, key = first[:, :width], jnp.concatenate((first[:, width:], second[:, width:]), axis=1)
    q_scale = lax.rsqrt(head_means(query * query, ones) + tiny_eps)
    k_scale = lax.rsqrt(head_means(key * key, ones) + tiny_eps)
    q_unit, k_unit = query * q_scale, key * k_scale
    q_half, k_half = q_unit.astype(bf16), k_unit.astype(bf16)
    v_half = second[:, :width].astype(bf16)
    grad_att = dot_nt(grads_ref[here, :], wo_ref[...]).astype(bf16)
    spans = []
    for low in range(0, STEP, SPAN):
        pairs = []
        for left in range(0, width, tile):
            at = (slice(low, low + SPAN), slice(left, left + tile))
            pairs.append(attention(q_half[at], k_half[at], v_half[at], grad_att[at], same_row))
        spans.append([jnp.concatenate(part, axis=1) for part in zip(*pairs)])
    attended, d_query, d_key, d_value = (jnp.concatenate(part, axis=0) for part in zip(*spans))
    att_ref[here, :] = attended
    d_query = (q_scale * (d_query - q_unit * head_means(q_unit * d_query, ones))).astype(bf16)
    d_key = (k_scale * (d_key - k_unit * head_means(k_unit * d_key, ones))).astype(bf16)
    d_ref[here, :width] = d_query
    d_ref[here, width:used] = d_key[:, :tile]
    d_ref[here, used : used + width] = d_value
    d_ref[here, used + width :] = d_key[:, tile:]

    @pl.when(step == pl.num_programs(0) - 1)
    def _():
        def sent_out(part):
            rows = pl.ds(part * depth, depth)
            return pltpu.make_async_copy(out_ref.at[rows], terms_ref.at[rows], sems.at[part])

        d_sent = pltpu.make_async_copy(d_ref, d_out_ref, sems.at[2])
        d_sent.start()
        out_terms = dot_tn(att_ref[...], grads_ref[...]).astype(bf16)
        for inner, outer in wo_parts():
            out_ref[outer] = out_terms[inner]
        out_ref[:depth, :used] = dot_tn(normed_ref[...], d_ref[:, :used]).astype(bf16)
        sent_out(0).start()
        out_ref[depth:, :used] = dot_tn(normed_ref[...], d_ref[:, used:]).astype(bf16)
        sent_out(1).start()
        d_sent.wait()
        sent_out(0).wait()
        sent_out(1).wait()


def layer(normed, grads, weights):
    tokens, depth = normed.shape

    def whole(shape):
        return pl.BlockSpec(shape, lambda i: (0, 0))

    outs = [(tokens, 3 * depth // 2), weights.shape]
    ins = (normed, grads, weights)
    return pl.pallas_call(
        layer_kernel,
        grid=(tokens // STEP,),
        in_specs=[whole(array.shape) for array in ins],
        out_specs=[pl.BlockSpec(memory_space=pltpu.HBM)] * 2,
        out_shape=[jax.ShapeDtypeStruct(shape, bf16) for shape in outs],
        scratch_shapes=[pltpu.VMEM(shape, bf16) for shape in outs]
        + [
            pltpu.VMEM((tokens, depth // 2), bf16),
            pltpu.VMEM((depth // 2, depth), bf16),
            pltpu.SemaphoreType.DMA((3,)),
        ],
        compiler_params=pltpu.CompilerParams(vmem_limit_bytes=40 * 1024 * 1024),
        cost_estimate=pl.CostEstimate(
            flops=10 * tokens * depth * depth, bytes_accessed=6 << 20, transcendentals=0
        ),
        name="attention_layer",
    )(*ins)


MESH_AXES = ("yh", "yl", "core", "x", "z")
ALL_Y = ("yh", "yl")
NEAR = ("yl", "x")


def swapped(block):
    return lax.ppermute(block, "core", [(0, 1), (1, 0)])


def sent(blocks, axis):
    return lax.all_to_all(blocks, axis, split_axis=0, concat_axis=0, tiled=True)


def blocks_of(terms, count):
    return terms.reshape(count, terms.shape[0] // count, terms.shape[1])


small = pltpu.CompilerParams(vmem_limit_bytes=8 * 1024 * 1024)


def head_lanes(shape):
    return lax.broadcasted_iota(jnp.int32, shape, 1) < HEAD


def core_heads(tiles, core):
    packed = []
    for low, high in zip(tiles[::2], tiles[1::2]):
        first = head_lanes(low.shape)
        moved = jnp.where(core == 0, high, low)
        kept = jnp.where(core == 0, low, high)
        moved = pltpu.roll(moved, HEAD, 1)
        packed.append(jnp.where(first == (core == 0), kept, moved))
    return jnp.concatenate(packed, axis=1)


def tiles_of(block):
    return [block[:, low : low + 2 * HEAD] for low in range(0, block.shape[1], 2 * HEAD)]


def copies_kernel(core_ref, yl_ref, wq_ref, wk_ref, wv_ref, wo_ref, out_ref):
    core = core_ref[0]
    width, tile = wq_ref.shape[1] // 2, 2 * HEAD

    def own(weight_ref):
        return core_heads(tiles_of(weight_ref[...].astype(f32)), core)

    for yl, first_ref in enumerate((wq_ref, wv_ref)):

        @pl.when(yl_ref[0] == yl)
        def _():
            low = 0
            for part in (
                own(first_ref),
                own(wk_ref)[:, yl * tile : (yl + 1) * tile],
                wo_ref[:, yl * width : (yl + 1) * width],
            ):
                out_ref[:, :, low : low + part.shape[1]] = jnp.broadcast_to(
                    part.astype(bf16)[None], (out_ref.shape[0],) + part.shape
                )
                low += part.shape[1]


def weight_copies(core, yl, weights, count):
    rows, width = weights[0].shape
    smem = pl.BlockSpec(memory_space=pltpu.SMEM)
    out = (count, rows, width + 2 * HEAD)
    return pl.pallas_call(
        copies_kernel,
        grid=(1,),
        in_specs=[smem, smem] + [pl.BlockSpec((rows, width), lambda i: (0, 0))] * 4,
        out_specs=pl.BlockSpec(out, lambda i: (0, 0, 0)),
        out_shape=jax.ShapeDtypeStruct(out, bf16),
        name="weight_copies",
    )(core, yl, *weights)


def lines_kernel(core_ref, blocks_ref, out_ref):
    count, rows, _ = blocks_ref.shape
    near, _, depth = out_ref.shape
    tile = 2 * HEAD
    used = depth - tile

    def write(low, part):
        out_ref[:, :, low : low + part.shape[1]] = jnp.broadcast_to(
            part[None], (near,) + part.shape
        )

    write(0, blocks_ref[:, :, :used].reshape(count * rows, used))
    heads = blocks_ref[pl.ds(core_ref[0] * (count // 2), count // 2), :, used:]
    heads = heads.reshape(count // 2 * rows, 2 * tile)
    write(used, jnp.concatenate((heads[:, :tile], heads[:, tile:]), axis=0))


def weight_lines(core, blocks, copies):
    count, rows, width = blocks.shape
    smem, vmem = (pl.BlockSpec(memory_space=space) for space in (pltpu.SMEM, pltpu.VMEM))
    return pl.pallas_call(
        lines_kernel,
        in_specs=[smem, vmem],
        out_specs=vmem,
        out_shape=jax.ShapeDtypeStruct((copies, count * rows, width - 2 * HEAD), bf16),
        compiler_params=small,
        name="weight_lines",
    )(core, blocks)


def near_sum_kernel(core_ref, blocks_ref, out_ref):
    total = jnp.sum(blocks_ref[...].astype(f32), axis=0).astype(bf16)
    count, rows, width = out_ref.shape
    tile = 2 * HEAD
    used = width - 2 * tile
    out_ref[:, :, :used] = total[:, :used].reshape(count, rows, used)
    out_ref[:, :, used:] = jnp.zeros((count, rows, 2 * tile), bf16)
    here = pl.ds(core_ref[0] * (count // 2), count // 2)
    heads = total[:, used:].reshape(2, count // 2, rows, tile)
    out_ref[here, :, used : used + tile] = heads[0]
    out_ref[here, :, used + tile :] = heads[1]


def near_sum(core, blocks, count):
    _, rows, depth = blocks.shape
    smem, vmem = (pl.BlockSpec(memory_space=space) for space in (pltpu.SMEM, pltpu.VMEM))
    return pl.pallas_call(
        near_sum_kernel,
        in_specs=[smem, vmem],
        out_specs=vmem,
        out_shape=jax.ShapeDtypeStruct((count, rows // count, depth + 2 * HEAD), bf16),
        compiler_params=small,
        name="near_sum",
    )(core, blocks)


def final_kernel(scale, blocks_ref, *out_refs):
    count, _, width = blocks_ref.shape
    tile = 2 * HEAD
    half = 2 * tile
    totals = []
    for place in range(4):
        total = blocks_ref[place].astype(f32)
        for yh in range(1, count // 4):
            total = total + blocks_ref[4 * yh + place].astype(f32)
        totals.append(total * scale)
    (first_a, first_b), (second_a, second_b) = totals[:2], totals[2:]
    for out_ref, pairs in (
        (out_refs[0], [(first_a, first_b, low) for low in (0, tile)]),
        (out_refs[1], [(first_a, first_b, half), (second_a, second_b, half)]),
        (out_refs[2], [(second_a, second_b, low) for low in (0, tile)]),
    ):
        at = 0
        for one, two, low in pairs:
            one, two = one[:, low : low + tile], two[:, low : low + tile]
            first = head_lanes(one.shape)
            for blended in ((one, pltpu.roll(two, HEAD, 1)), (pltpu.roll(one, HEAD, 1), two)):
                out_ref[:, at : at + tile] = jnp.where(first, *blended)
                at += tile
    for yl, (one, two) in enumerate(((first_a, first_b), (second_a, second_b))):
        out_refs[3][:, yl * half : (yl + 1) * half] = one[:, half + tile :] + two[:, half + tile :]


def final_sum(blocks, scale):
    _, rows, width = blocks.shape
    width = width - 2 * HEAD
    vmem = pl.BlockSpec(memory_space=pltpu.VMEM)
    return pl.pallas_call(
        functools.partial(final_kernel, scale),
        in_specs=[vmem],
        out_specs=[vmem] * 4,
        out_shape=[jax.ShapeDtypeStruct((rows, width), f32)] * 4,
        compiler_params=small,
        name="final_sum",
    )(blocks)


def local(trace_rows, upstream, counts, w_query, w_key, w_value, w_out):
    core, yl = lax.axis_index("core").reshape(1), lax.axis_index("yl").reshape(1)
    view_count, most_rows, row_length, depth = trace_rows.shape
    tokens = view_count * most_rows * row_length
    view_counts = counts.reshape(view_count)

    copies = weight_copies(core, yl, (w_query, w_key, w_value, w_out), lax.axis_size("z"))
    rows, up = trace_rows.reshape(tokens, depth), upstream.reshape(tokens, depth)
    is_live = lax.iota(jnp.int32, most_rows)[None, :] < view_counts[:, None]
    is_live = jnp.repeat(is_live.reshape(-1), row_length)[:, None]
    masked = jnp.where(is_live, up, jnp.zeros((), up.dtype))
    blocks = sent(copies, "z")
    lines = weight_lines(core, blocks, lax.axis_size(NEAR))
    weights = sent(lines, NEAR).reshape(-1, depth)

    both_rows = jnp.concatenate((rows, swapped(rows)), axis=0).astype(f32)
    both_masked = jnp.concatenate((masked, swapped(masked)), axis=0)
    inv_rms = lax.rsqrt(jnp.mean(both_rows * both_rows, axis=-1, keepdims=True) + tiny_eps)
    normed = (both_rows * inv_rms).astype(bf16)
    d_qkv, terms = layer(normed, both_masked, weights)

    z_count = lax.axis_size("z")
    total = near_sum(core, sent(blocks_of(terms, lax.axis_size(NEAR)), NEAR), z_count)
    total = jnp.sum(sent(total, "z").astype(f32), axis=0).astype(bf16)
    total = jnp.broadcast_to(total[None], (lax.axis_size(ALL_Y + ("core",)),) + total.shape)
    devices = math.prod(lax.axis_size(name) for name in MESH_AXES)
    weight_grads = final_sum(
        sent(total, ALL_Y + ("core",)), 1.0 / math.sqrt(devices * tokens // 2)
    )

    used = d_qkv.shape[1] // 2
    grad_norm = dot_nt(d_qkv[:, :used], weights[:depth, :used]) + dot_nt(
        d_qkv[:, used:], weights[depth:, :used]
    )
    grad_norm = grad_norm[:tokens] + swapped(grad_norm[tokens:].astype(bf16)).astype(f32)
    inv_rms = inv_rms[:tokens]
    scaled = both_rows[:tokens] * inv_rms
    done = masked.astype(f32) + inv_rms * (
        grad_norm - scaled * jnp.mean(scaled * grad_norm, axis=-1, keepdims=True)
    )
    return (done.astype(bf16).reshape(trace_rows.shape), *weight_grads)


def solution(mesh):
    fine_mesh = jax.sharding.Mesh(mesh.devices.reshape(4, 2, 2, 4, 8), MESH_AXES)
    every, peer = P(MESH_AXES), P(("x", "z"), None)
    in_specs = (every, every, P(("yh", "yl", "core"), ("x", "z")), peer, peer, peer, peer)
    out_specs = (every, peer, peer, peer, peer)
    return jax.shard_map(
        local, mesh=fine_mesh, in_specs=in_specs, out_specs=out_specs, check_vma=False
    )
```

```python
import functools
import math
import jax
import jax.numpy as jnp
from jax import lax
from jax.experimental import pallas as pl
from jax.experimental.pallas import tpu as pltpu
from jax.sharding import PartitionSpec as P

HEAD = 64
ROW = 32
SPAN = 128
STEP = 512
gain = 6.0 / HEAD
tiny_eps = 1e-06
f32, bf16 = jnp.float32, jnp.bfloat16


def dot_nn(a, b):
    return lax.dot_general(a, b, (((1,), (0,)), ((), ())), preferred_element_type=f32)


def dot_nt(a, b):
    return lax.dot_general(a, b, (((1,), (1,)), ((), ())), preferred_element_type=f32)


def dot_tn(a, b):
    return lax.dot_general(a, b, (((0,), (0,)), ((), ())), preferred_element_type=f32)


def head_ones(width):
    row = lax.broadcasted_iota(jnp.int32, (width, width), 0) // HEAD
    col = lax.broadcasted_iota(jnp.int32, (width, width), 1) // HEAD
    return jnp.where(row == col, 1.0, 0.0).astype(bf16)


def head_means(values, ones):
    return dot_nn(values.astype(bf16), ones) * (1.0 / HEAD)


def stacked(block):
    first = lax.broadcasted_iota(jnp.int32, block.shape, 1) < HEAD
    zero = jnp.zeros((), block.dtype)
    return jnp.concatenate((jnp.where(first, block, zero), jnp.where(first, zero, block)), axis=0)


def unstacked(block):
    span = block.shape[0] // 2
    first = lax.broadcasted_iota(jnp.int32, (span, block.shape[1]), 1) < HEAD
    return jnp.where(first, block[:span], block[span:])


def scores_of(q_half, k_two, v_two, grad_att):
    return dot_nt(k_two, q_half), dot_nt(v_two, grad_att)


def softmax_of(scores, grad_probs, same_row):
    exps = jnp.where(same_row, jnp.exp(scores * gain), 0.0)
    probs, d_scores = [], []
    for half in (slice(0, SPAN), slice(SPAN, 2 * SPAN)):
        part = exps[half] * (1.0 / jnp.sum(exps[half], axis=0, keepdims=True))
        weighted = part * grad_probs[half]
        total = jnp.sum(weighted, axis=0, keepdims=True)
        probs.append(part.astype(bf16))
        d_scores.append(((weighted - part * total) * gain).astype(bf16))
    return jnp.concatenate(probs, axis=0), jnp.concatenate(d_scores, axis=0)


def attention(blocks, same_row):
    twos = [(stacked(k_half), stacked(v_half)) for _, k_half, v_half, _ in blocks]
    scores = [
        scores_of(q_half, *two, grad_att) for (q_half, _, _, grad_att), two in zip(blocks, twos)
    ]
    parts = [softmax_of(*pair, same_row) for pair in scores]
    return [
        (
            dot_tn(probs, v_two).astype(bf16),
            dot_tn(d_scores, k_two),
            unstacked(dot_nn(d_scores, q_half)),
            unstacked(dot_nn(probs, grad_att)).astype(bf16),
        )
        for (q_half, _, _, grad_att), (k_two, v_two), (probs, d_scores) in zip(blocks, twos, parts)
    ]


def layer_kernel(
    normed_ref, grads_ref, weights_ref, d_out_ref, terms_ref, d_ref, out_ref, att_ref, wo_ref, sems
):
    step = pl.program_id(0)
    depth = normed_ref.shape[1]
    width, tile = depth // 2, 2 * HEAD
    used = width + tile
    here = pl.ds(pl.multiple_of(step * STEP, STEP), STEP)

    def wo_parts():
        for low in range(0, width, HEAD):
            for part in range(4):
                at = part // 2 * depth + 2 * low + part % 2 * HEAD
                rows, cols = slice(low, low + HEAD), slice(part * tile, (part + 1) * tile)
                yield (rows, cols), (slice(at, at + HEAD), slice(used, depth))

    @pl.when(step == 0)
    def _():
        for inner, outer in wo_parts():
            wo_ref[inner] = weights_ref[outer]

    ones = head_ones(width)
    normed = normed_ref[here, :]
    row_of = lax.broadcasted_iota(jnp.int32, (2 * SPAN, SPAN), 0) % SPAN // ROW
    col_of = lax.broadcasted_iota(jnp.int32, (2 * SPAN, SPAN), 1) // ROW
    same_row = row_of == col_of

    first = dot_nn(normed, weights_ref[:depth, :used])
    second = dot_nn(normed, weights_ref[depth:, :used])
    query, key = first[:, :width], jnp.concatenate((first[:, width:], second[:, width:]), axis=1)
    q_scale = lax.rsqrt(head_means(query * query, ones) + tiny_eps)
    k_scale = lax.rsqrt(head_means(key * key, ones) + tiny_eps)
    q_unit, k_unit = query * q_scale, key * k_scale
    q_half, k_half = q_unit.astype(bf16), k_unit.astype(bf16)
    v_half = second[:, :width].astype(bf16)
    grad_att = dot_nt(grads_ref[here, :], wo_ref[...]).astype(bf16)
    places = [
        (slice(low, low + SPAN), slice(left, left + tile))
        for low in range(0, STEP, SPAN)
        for left in range(0, width, tile)
    ]
    found = attention(
        [(q_half[at], k_half[at], v_half[at], grad_att[at]) for at in places], same_row
    )
    spans = [
        [jnp.concatenate(part, axis=1) for part in zip(*found[i : i + 2])]
        for i in range(0, len(found), 2)
    ]
    attended, d_query, d_key, d_value = (jnp.concatenate(part, axis=0) for part in zip(*spans))
    att_ref[here, :] = attended
    d_query = (q_scale * (d_query - q_unit * head_means(q_unit * d_query, ones))).astype(bf16)
    d_key = (k_scale * (d_key - k_unit * head_means(k_unit * d_key, ones))).astype(bf16)
    d_ref[here, :width] = d_query
    d_ref[here, width:used] = d_key[:, :tile]
    d_ref[here, used : used + width] = d_value
    d_ref[here, used + width :] = d_key[:, tile:]

    @pl.when(step == pl.num_programs(0) - 1)
    def _():
        def sent_out(part):
            rows = pl.ds(part * depth, depth)
            return pltpu.make_async_copy(out_ref.at[rows], terms_ref.at[rows], sems.at[part])

        d_sent = pltpu.make_async_copy(d_ref, d_out_ref, sems.at[2])
        d_sent.start()
        out_terms = dot_tn(att_ref[...], grads_ref[...]).astype(bf16)
        for inner, outer in wo_parts():
            out_ref[outer] = out_terms[inner]
        out_ref[:depth, :used] = dot_tn(normed_ref[...], d_ref[:, :used]).astype(bf16)
        sent_out(0).start()
        out_ref[depth:, :used] = dot_tn(normed_ref[...], d_ref[:, used:]).astype(bf16)
        sent_out(1).start()
        d_sent.wait()
        sent_out(0).wait()
        sent_out(1).wait()


def layer(normed, grads, weights):
    tokens, depth = normed.shape

    def whole(shape):
        return pl.BlockSpec(shape, lambda i: (0, 0))

    outs = [(tokens, 3 * depth // 2), weights.shape]
    ins = (normed, grads, weights)
    return pl.pallas_call(
        layer_kernel,
        grid=(tokens // STEP,),
        in_specs=[whole(array.shape) for array in ins],
        out_specs=[pl.BlockSpec(memory_space=pltpu.HBM)] * 2,
        out_shape=[jax.ShapeDtypeStruct(shape, bf16) for shape in outs],
        scratch_shapes=[pltpu.VMEM(shape, bf16) for shape in outs]
        + [
            pltpu.VMEM((tokens, depth // 2), bf16),
            pltpu.VMEM((depth // 2, depth), bf16),
            pltpu.SemaphoreType.DMA((3,)),
        ],
        compiler_params=pltpu.CompilerParams(vmem_limit_bytes=40 * 1024 * 1024),
        cost_estimate=pl.CostEstimate(
            flops=10 * tokens * depth * depth, bytes_accessed=6 << 20, transcendentals=0
        ),
        name="attention_layer",
    )(*ins)


MESH_AXES = ("yh", "yl", "core", "x", "z")
ALL_Y = ("yh", "yl")
NEAR = ("yl", "x")


def swapped(block):
    return lax.ppermute(block, "core", [(0, 1), (1, 0)])


def sent(blocks, axis):
    return lax.all_to_all(blocks, axis, split_axis=0, concat_axis=0, tiled=True)


def blocks_of(terms, count):
    return terms.reshape(count, terms.shape[0] // count, terms.shape[1])


small = pltpu.CompilerParams(vmem_limit_bytes=8 * 1024 * 1024)


def head_lanes(shape):
    return lax.broadcasted_iota(jnp.int32, shape, 1) < HEAD


def core_heads(tiles, core):
    packed = []
    for low, high in zip(tiles[::2], tiles[1::2]):
        first = head_lanes(low.shape)
        moved = jnp.where(core == 0, high, low)
        kept = jnp.where(core == 0, low, high)
        moved = pltpu.roll(moved, HEAD, 1)
        packed.append(jnp.where(first == (core == 0), kept, moved))
    return jnp.concatenate(packed, axis=1)


def tiles_of(block):
    return [block[:, low : low + 2 * HEAD] for low in range(0, block.shape[1], 2 * HEAD)]


def copies_kernel(core_ref, yl_ref, wq_ref, wk_ref, wv_ref, wo_ref, out_ref):
    core = core_ref[0]
    width, tile = wq_ref.shape[1] // 2, 2 * HEAD

    def own(weight_ref):
        return core_heads(tiles_of(weight_ref[...].astype(f32)), core)

    for yl, first_ref in enumerate((wq_ref, wv_ref)):

        @pl.when(yl_ref[0] == yl)
        def _():
            low = 0
            for part in (
                own(first_ref),
                own(wk_ref)[:, yl * tile : (yl + 1) * tile],
                wo_ref[:, yl * width : (yl + 1) * width],
            ):
                out_ref[:, :, low : low + part.shape[1]] = jnp.broadcast_to(
                    part.astype(bf16)[None], (out_ref.shape[0],) + part.shape
                )
                low += part.shape[1]


def weight_copies(core, yl, weights, count):
    rows, width = weights[0].shape
    smem = pl.BlockSpec(memory_space=pltpu.SMEM)
    out = (count, rows, width + 2 * HEAD)
    return pl.pallas_call(
        copies_kernel,
        grid=(1,),
        in_specs=[smem, smem] + [pl.BlockSpec((rows, width), lambda i: (0, 0))] * 4,
        out_specs=pl.BlockSpec(out, lambda i: (0, 0, 0)),
        out_shape=jax.ShapeDtypeStruct(out, bf16),
        name="weight_copies",
    )(core, yl, *weights)


def lines_kernel(core_ref, blocks_ref, out_ref):
    count, rows, _ = blocks_ref.shape
    near, _, depth = out_ref.shape
    tile = 2 * HEAD
    used = depth - tile

    def write(low, part):
        out_ref[:, :, low : low + part.shape[1]] = jnp.broadcast_to(
            part[None], (near,) + part.shape
        )

    write(0, blocks_ref[:, :, :used].reshape(count * rows, used))
    heads = blocks_ref[pl.ds(core_ref[0] * (count // 2), count // 2), :, used:]
    heads = heads.reshape(count // 2 * rows, 2 * tile)
    write(used, jnp.concatenate((heads[:, :tile], heads[:, tile:]), axis=0))


def weight_lines(core, blocks, copies):
    count, rows, width = blocks.shape
    smem, vmem = (pl.BlockSpec(memory_space=space) for space in (pltpu.SMEM, pltpu.VMEM))
    return pl.pallas_call(
        lines_kernel,
        in_specs=[smem, vmem],
        out_specs=vmem,
        out_shape=jax.ShapeDtypeStruct((copies, count * rows, width - 2 * HEAD), bf16),
        compiler_params=small,
        name="weight_lines",
    )(core, blocks)


def near_sum_kernel(core_ref, blocks_ref, out_ref):
    total = jnp.sum(blocks_ref[...].astype(f32), axis=0).astype(bf16)
    count, rows, width = out_ref.shape
    tile = 2 * HEAD
    used = width - 2 * tile
    out_ref[:, :, :used] = total[:, :used].reshape(count, rows, used)
    out_ref[:, :, used:] = jnp.zeros((count, rows, 2 * tile), bf16)
    here = pl.ds(core_ref[0] * (count // 2), count // 2)
    heads = total[:, used:].reshape(2, count // 2, rows, tile)
    out_ref[here, :, used : used + tile] = heads[0]
    out_ref[here, :, used + tile :] = heads[1]


def near_sum(core, blocks, count):
    _, rows, depth = blocks.shape
    smem, vmem = (pl.BlockSpec(memory_space=space) for space in (pltpu.SMEM, pltpu.VMEM))
    return pl.pallas_call(
        near_sum_kernel,
        in_specs=[smem, vmem],
        out_specs=vmem,
        out_shape=jax.ShapeDtypeStruct((count, rows // count, depth + 2 * HEAD), bf16),
        compiler_params=small,
        name="near_sum",
    )(core, blocks)


def final_kernel(scale, blocks_ref, *out_refs):
    count, _, width = blocks_ref.shape
    tile = 2 * HEAD
    half = 2 * tile
    totals = []
    for place in range(4):
        total = blocks_ref[place].astype(f32)
        for yh in range(1, count // 4):
            total = total + blocks_ref[4 * yh + place].astype(f32)
        totals.append(total * scale)
    (first_a, first_b), (second_a, second_b) = totals[:2], totals[2:]
    for out_ref, pairs in (
        (out_refs[0], [(first_a, first_b, low) for low in (0, tile)]),
        (out_refs[1], [(first_a, first_b, half), (second_a, second_b, half)]),
        (out_refs[2], [(second_a, second_b, low) for low in (0, tile)]),
    ):
        at = 0
        for one, two, low in pairs:
            one, two = one[:, low : low + tile], two[:, low : low + tile]
            first = head_lanes(one.shape)
            for blended in ((one, pltpu.roll(two, HEAD, 1)), (pltpu.roll(one, HEAD, 1), two)):
                out_ref[:, at : at + tile] = jnp.where(first, *blended)
                at += tile
    for yl, (one, two) in enumerate(((first_a, first_b), (second_a, second_b))):
        out_refs[3][:, yl * half : (yl + 1) * half] = one[:, half + tile :] + two[:, half + tile :]


def final_sum(blocks, scale):
    _, rows, width = blocks.shape
    width = width - 2 * HEAD
    vmem = pl.BlockSpec(memory_space=pltpu.VMEM)
    return pl.pallas_call(
        functools.partial(final_kernel, scale),
        in_specs=[vmem],
        out_specs=[vmem] * 4,
        out_shape=[jax.ShapeDtypeStruct((rows, width), f32)] * 4,
        compiler_params=small,
        name="final_sum",
    )(blocks)


def local(trace_rows, upstream, counts, w_query, w_key, w_value, w_out):
    core, yl = lax.axis_index("core").reshape(1), lax.axis_index("yl").reshape(1)
    view_count, most_rows, row_length, depth = trace_rows.shape
    tokens = view_count * most_rows * row_length
    view_counts = counts.reshape(view_count)

    copies = weight_copies(core, yl, (w_query, w_key, w_value, w_out), lax.axis_size("z"))
    rows, up = trace_rows.reshape(tokens, depth), upstream.reshape(tokens, depth)
    is_live = lax.iota(jnp.int32, most_rows)[None, :] < view_counts[:, None]
    is_live = jnp.repeat(is_live.reshape(-1), row_length)[:, None]
    masked = jnp.where(is_live, up, jnp.zeros((), up.dtype))
    blocks = sent(copies, "z")
    lines = weight_lines(core, blocks, lax.axis_size(NEAR))
    weights = sent(lines, NEAR).reshape(-1, depth)

    both_rows = jnp.concatenate((rows, swapped(rows)), axis=0).astype(f32)
    both_masked = jnp.concatenate((masked, swapped(masked)), axis=0)
    inv_rms = lax.rsqrt(jnp.mean(both_rows * both_rows, axis=-1, keepdims=True) + tiny_eps)
    normed = (both_rows * inv_rms).astype(bf16)
    d_qkv, terms = layer(normed, both_masked, weights)

    z_count = lax.axis_size("z")
    total = near_sum(core, sent(blocks_of(terms, lax.axis_size(NEAR)), NEAR), z_count)
    total = jnp.sum(sent(total, "z").astype(f32), axis=0).astype(bf16)
    total = jnp.broadcast_to(total[None], (lax.axis_size(ALL_Y + ("core",)),) + total.shape)
    devices = math.prod(lax.axis_size(name) for name in MESH_AXES)
    weight_grads = final_sum(
        sent(total, ALL_Y + ("core",)), 1.0 / math.sqrt(devices * tokens // 2)
    )

    used = d_qkv.shape[1] // 2
    grad_norm = dot_nt(d_qkv[:, :used], weights[:depth, :used]) + dot_nt(
        d_qkv[:, used:], weights[depth:, :used]
    )
    grad_norm = grad_norm[:tokens] + swapped(grad_norm[tokens:].astype(bf16)).astype(f32)
    inv_rms = inv_rms[:tokens]
    scaled = both_rows[:tokens] * inv_rms
    done = masked.astype(f32) + inv_rms * (
        grad_norm - scaled * jnp.mean(scaled * grad_norm, axis=-1, keepdims=True)
    )
    return (done.astype(bf16).reshape(trace_rows.shape), *weight_grads)


def solution(mesh):
    fine_mesh = jax.sharding.Mesh(mesh.devices.reshape(4, 2, 2, 4, 8), MESH_AXES)
    every, peer = P(MESH_AXES), P(("x", "z"), None)
    in_specs = (every, every, P(("yh", "yl", "core"), ("x", "z")), peer, peer, peer, peer)
    out_specs = (every, peer, peer, peer, peer)
    return jax.shard_map(
        local, mesh=fine_mesh, in_specs=in_specs, out_specs=out_specs, check_vma=False
    )
```

```python
import functools
import math
import jax
import jax.numpy as jnp
from jax import lax
from jax.experimental import pallas as pl
from jax.experimental.pallas import tpu as pltpu
from jax.sharding import PartitionSpec as P

HEAD = 64
ROW = 32
SPAN = 128
STEP = 512
gain = 6.0 / HEAD
tiny_eps = 1e-06
f32, bf16 = jnp.float32, jnp.bfloat16


def dot_nn(a, b):
    return lax.dot_general(a, b, (((1,), (0,)), ((), ())), preferred_element_type=f32)


def dot_nt(a, b):
    return lax.dot_general(a, b, (((1,), (1,)), ((), ())), preferred_element_type=f32)


def dot_tn(a, b):
    return lax.dot_general(a, b, (((0,), (0,)), ((), ())), preferred_element_type=f32)


def head_ones(width):
    row = lax.broadcasted_iota(jnp.int32, (width, width), 0) // HEAD
    col = lax.broadcasted_iota(jnp.int32, (width, width), 1) // HEAD
    return jnp.where(row == col, 1.0, 0.0).astype(bf16)


def head_means(values, ones):
    return dot_nn(values.astype(bf16), ones) * (1.0 / HEAD)


def stacked(block):
    first = lax.broadcasted_iota(jnp.int32, block.shape, 1) < HEAD
    zero = jnp.zeros((), block.dtype)
    return jnp.concatenate((jnp.where(first, block, zero), jnp.where(first, zero, block)), axis=0)


def unstacked(block):
    span = block.shape[0] // 2
    first = lax.broadcasted_iota(jnp.int32, (span, block.shape[1]), 1) < HEAD
    return jnp.where(first, block[:span], block[span:])


def scores_of(q_half, k_two, v_two, grad_att):
    return dot_nt(k_two, q_half), dot_nt(v_two, grad_att)


def softmax_of(scores, grad_probs, same_row):
    exps = jnp.where(same_row, jnp.exp(scores * gain), 0.0)
    probs, d_scores = [], []
    for half in (slice(0, SPAN), slice(SPAN, 2 * SPAN)):
        part = exps[half] * (1.0 / jnp.sum(exps[half], axis=0, keepdims=True))
        weighted = part * grad_probs[half]
        total = jnp.sum(weighted, axis=0, keepdims=True)
        probs.append(part.astype(bf16))
        d_scores.append(((weighted - part * total) * gain).astype(bf16))
    return jnp.concatenate(probs, axis=0), jnp.concatenate(d_scores, axis=0)


def attention(blocks, same_row):
    twos = [(stacked(k_half), stacked(v_half)) for _, k_half, v_half, _ in blocks]
    scores = [
        scores_of(q_half, *two, grad_att) for (q_half, _, _, grad_att), two in zip(blocks, twos)
    ]
    parts = [softmax_of(*pair, same_row) for pair in scores]
    return [
        (
            dot_tn(probs, v_two).astype(bf16),
            dot_tn(d_scores, k_two),
            unstacked(dot_nn(d_scores, q_half)),
            unstacked(dot_nn(probs, grad_att)).astype(bf16),
        )
        for (q_half, _, _, grad_att), (k_two, v_two), (probs, d_scores) in zip(blocks, twos, parts)
    ]


def layer_kernel(
    normed_ref, grads_ref, weights_ref, d_out_ref, terms_ref, d_ref, out_ref, att_ref, wo_ref, sems
):
    step = pl.program_id(0)
    depth = normed_ref.shape[1]
    width, tile = depth // 2, 2 * HEAD
    used = width + tile
    here = pl.ds(pl.multiple_of(step * STEP, STEP), STEP)

    def wo_parts():
        for low in range(0, width, HEAD):
            for part in range(4):
                at = part // 2 * depth + 2 * low + part % 2 * HEAD
                rows, cols = slice(low, low + HEAD), slice(part * tile, (part + 1) * tile)
                yield (rows, cols), (slice(at, at + HEAD), slice(used, depth))

    @pl.when(step == 0)
    def _():
        for inner, outer in wo_parts():
            wo_ref[inner] = weights_ref[outer]

    ones = head_ones(width)
    normed = normed_ref[here, :]
    row_of = lax.broadcasted_iota(jnp.int32, (2 * SPAN, SPAN), 0) % SPAN // ROW
    col_of = lax.broadcasted_iota(jnp.int32, (2 * SPAN, SPAN), 1) // ROW
    same_row = row_of == col_of

    first = dot_nn(normed, weights_ref[:depth, :used])
    second = dot_nn(normed, weights_ref[depth:, :used])
    query, key = first[:, :width], jnp.concatenate((first[:, width:], second[:, width:]), axis=1)
    q_scale = lax.rsqrt(head_means(query * query, ones) + tiny_eps)
    k_scale = lax.rsqrt(head_means(key * key, ones) + tiny_eps)
    q_unit, k_unit = query * q_scale, key * k_scale
    q_half, k_half = q_unit.astype(bf16), k_unit.astype(bf16)
    v_half = second[:, :width].astype(bf16)
    grad_att = dot_nt(grads_ref[here, :], wo_ref[...]).astype(bf16)
    places = [
        (slice(low, low + SPAN), slice(left, left + tile))
        for low in range(0, STEP, SPAN)
        for left in range(0, width, tile)
    ]
    found = attention(
        [(q_half[at], k_half[at], v_half[at], grad_att[at]) for at in places], same_row
    )
    spans = [
        [jnp.concatenate(part, axis=1) for part in zip(*found[i : i + 2])]
        for i in range(0, len(found), 2)
    ]
    attended, d_query, d_key, d_value = (jnp.concatenate(part, axis=0) for part in zip(*spans))
    att_ref[here, :] = attended
    d_query = (q_scale * (d_query - q_unit * head_means(q_unit * d_query, ones))).astype(bf16)
    d_key = (k_scale * (d_key - k_unit * head_means(k_unit * d_key, ones))).astype(bf16)
    d_ref[here, :width] = d_query
    d_ref[here, width:used] = d_key[:, :tile]
    d_ref[here, used : used + width] = d_value
    d_ref[here, used + width :] = d_key[:, tile:]

    @pl.when(step == pl.num_programs(0) - 1)
    def _():
        def sent_out(part):
            rows = pl.ds(part * depth, depth)
            return pltpu.make_async_copy(out_ref.at[rows], terms_ref.at[rows], sems.at[part])

        d_sent = pltpu.make_async_copy(d_ref, d_out_ref, sems.at[2])
        d_sent.start()
        out_terms = dot_tn(att_ref[...], grads_ref[...]).astype(bf16)
        for inner, outer in wo_parts():
            out_ref[outer] = out_terms[inner]
        out_ref[:depth, :used] = dot_tn(normed_ref[...], d_ref[:, :used]).astype(bf16)
        sent_out(0).start()
        out_ref[depth:, :used] = dot_tn(normed_ref[...], d_ref[:, used:]).astype(bf16)
        sent_out(1).start()
        d_sent.wait()
        sent_out(0).wait()
        sent_out(1).wait()


def layer(normed, grads, weights):
    tokens, depth = normed.shape

    def whole(shape):
        return pl.BlockSpec(shape, lambda i: (0, 0))

    outs = [(tokens, 3 * depth // 2), weights.shape]
    ins = (normed, grads, weights)
    return pl.pallas_call(
        layer_kernel,
        grid=(tokens // STEP,),
        in_specs=[whole(array.shape) for array in ins],
        out_specs=[pl.BlockSpec(memory_space=pltpu.HBM)] * 2,
        out_shape=[pltpu.HBM(shape, bf16) for shape in outs],
        scratch_shapes=[pltpu.VMEM(shape, bf16) for shape in outs]
        + [
            pltpu.VMEM((tokens, depth // 2), bf16),
            pltpu.VMEM((depth // 2, depth), bf16),
            pltpu.SemaphoreType.DMA((3,)),
        ],
        compiler_params=pltpu.CompilerParams(vmem_limit_bytes=40 * 1024 * 1024),
        cost_estimate=pl.CostEstimate(
            flops=10 * tokens * depth * depth, bytes_accessed=6 << 20, transcendentals=0
        ),
        name="attention_layer",
    )(*ins)


MESH_AXES = ("yh", "yl", "core", "x", "z")
ALL_Y = ("yh", "yl")
NEAR = ("yl", "x")


def swapped(block):
    return lax.ppermute(block, "core", [(0, 1), (1, 0)])


def sent(blocks, axis):
    return lax.all_to_all(blocks, axis, split_axis=0, concat_axis=0, tiled=True)


def blocks_of(terms, count):
    return terms.reshape(count, terms.shape[0] // count, terms.shape[1])


small = pltpu.CompilerParams(vmem_limit_bytes=8 * 1024 * 1024)


def head_lanes(shape):
    return lax.broadcasted_iota(jnp.int32, shape, 1) < HEAD


def core_heads(tiles, core):
    packed = []
    for low, high in zip(tiles[::2], tiles[1::2]):
        first = head_lanes(low.shape)
        moved = jnp.where(core == 0, high, low)
        kept = jnp.where(core == 0, low, high)
        moved = pltpu.roll(moved, HEAD, 1)
        packed.append(jnp.where(first == (core == 0), kept, moved))
    return jnp.concatenate(packed, axis=1)


def tiles_of(block):
    return [block[:, low : low + 2 * HEAD] for low in range(0, block.shape[1], 2 * HEAD)]


def copies_kernel(core_ref, yl_ref, wq_ref, wk_ref, wv_ref, wo_ref, out_ref):
    core = core_ref[0]
    width, tile = wq_ref.shape[1] // 2, 2 * HEAD

    def own(weight_ref):
        return core_heads(tiles_of(weight_ref[...].astype(f32)), core)

    for yl, first_ref in enumerate((wq_ref, wv_ref)):

        @pl.when(yl_ref[0] == yl)
        def _():
            low = 0
            for part in (
                own(first_ref),
                own(wk_ref)[:, yl * tile : (yl + 1) * tile],
                wo_ref[:, yl * width : (yl + 1) * width],
            ):
                out_ref[:, :, low : low + part.shape[1]] = jnp.broadcast_to(
                    part.astype(bf16)[None], (out_ref.shape[0],) + part.shape
                )
                low += part.shape[1]


def weight_copies(core, yl, weights, count):
    rows, width = weights[0].shape
    smem = pl.BlockSpec(memory_space=pltpu.SMEM)
    out = (count, rows, width + 2 * HEAD)
    return pl.pallas_call(
        copies_kernel,
        grid=(1,),
        in_specs=[smem, smem] + [pl.BlockSpec((rows, width), lambda i: (0, 0))] * 4,
        out_specs=pl.BlockSpec(out, lambda i: (0, 0, 0)),
        out_shape=jax.ShapeDtypeStruct(out, bf16),
        name="weight_copies",
    )(core, yl, *weights)


def lines_kernel(core_ref, blocks_ref, out_ref):
    count, rows, _ = blocks_ref.shape
    near, _, depth = out_ref.shape
    tile = 2 * HEAD
    used = depth - tile

    def write(low, part):
        out_ref[:, :, low : low + part.shape[1]] = jnp.broadcast_to(
            part[None], (near,) + part.shape
        )

    write(0, blocks_ref[:, :, :used].reshape(count * rows, used))
    heads = blocks_ref[pl.ds(core_ref[0] * (count // 2), count // 2), :, used:]
    heads = heads.reshape(count // 2 * rows, 2 * tile)
    write(used, jnp.concatenate((heads[:, :tile], heads[:, tile:]), axis=0))


def weight_lines(core, blocks, copies):
    count, rows, width = blocks.shape
    smem, vmem = (pl.BlockSpec(memory_space=space) for space in (pltpu.SMEM, pltpu.VMEM))
    return pl.pallas_call(
        lines_kernel,
        in_specs=[smem, vmem],
        out_specs=vmem,
        out_shape=jax.ShapeDtypeStruct((copies, count * rows, width - 2 * HEAD), bf16),
        compiler_params=small,
        name="weight_lines",
    )(core, blocks)


def near_sum_kernel(core_ref, blocks_ref, out_ref):
    total = jnp.sum(blocks_ref[...].astype(f32), axis=0).astype(bf16)
    count, rows, width = out_ref.shape
    tile = 2 * HEAD
    used = width - 2 * tile
    out_ref[:, :, :used] = total[:, :used].reshape(count, rows, used)
    out_ref[:, :, used:] = jnp.zeros((count, rows, 2 * tile), bf16)
    here = pl.ds(core_ref[0] * (count // 2), count // 2)
    heads = total[:, used:].reshape(2, count // 2, rows, tile)
    out_ref[here, :, used : used + tile] = heads[0]
    out_ref[here, :, used + tile :] = heads[1]


def near_sum(core, blocks, count):
    _, rows, depth = blocks.shape
    smem, vmem = (pl.BlockSpec(memory_space=space) for space in (pltpu.SMEM, pltpu.VMEM))
    return pl.pallas_call(
        near_sum_kernel,
        in_specs=[smem, vmem],
        out_specs=vmem,
        out_shape=jax.ShapeDtypeStruct((count, rows // count, depth + 2 * HEAD), bf16),
        compiler_params=small,
        name="near_sum",
    )(core, blocks)


def final_kernel(scale, blocks_ref, *out_refs):
    count, _, width = blocks_ref.shape
    tile = 2 * HEAD
    half = 2 * tile
    totals = []
    for place in range(4):
        total = blocks_ref[place].astype(f32)
        for yh in range(1, count // 4):
            total = total + blocks_ref[4 * yh + place].astype(f32)
        totals.append(total * scale)
    (first_a, first_b), (second_a, second_b) = totals[:2], totals[2:]
    for out_ref, pairs in (
        (out_refs[0], [(first_a, first_b, low) for low in (0, tile)]),
        (out_refs[1], [(first_a, first_b, half), (second_a, second_b, half)]),
        (out_refs[2], [(second_a, second_b, low) for low in (0, tile)]),
    ):
        at = 0
        for one, two, low in pairs:
            one, two = one[:, low : low + tile], two[:, low : low + tile]
            first = head_lanes(one.shape)
            for blended in ((one, pltpu.roll(two, HEAD, 1)), (pltpu.roll(one, HEAD, 1), two)):
                out_ref[:, at : at + tile] = jnp.where(first, *blended)
                at += tile
    for yl, (one, two) in enumerate(((first_a, first_b), (second_a, second_b))):
        out_refs[3][:, yl * half : (yl + 1) * half] = one[:, half + tile :] + two[:, half + tile :]


def final_sum(blocks, scale):
    _, rows, width = blocks.shape
    width = width - 2 * HEAD
    vmem = pl.BlockSpec(memory_space=pltpu.VMEM)
    return pl.pallas_call(
        functools.partial(final_kernel, scale),
        in_specs=[vmem],
        out_specs=[vmem] * 4,
        out_shape=[jax.ShapeDtypeStruct((rows, width), f32)] * 4,
        compiler_params=small,
        name="final_sum",
    )(blocks)


def local(trace_rows, upstream, counts, w_query, w_key, w_value, w_out):
    core, yl = lax.axis_index("core").reshape(1), lax.axis_index("yl").reshape(1)
    view_count, most_rows, row_length, depth = trace_rows.shape
    tokens = view_count * most_rows * row_length
    view_counts = counts.reshape(view_count)

    copies = weight_copies(core, yl, (w_query, w_key, w_value, w_out), lax.axis_size("z"))
    rows, up = trace_rows.reshape(tokens, depth), upstream.reshape(tokens, depth)
    is_live = lax.iota(jnp.int32, most_rows)[None, :] < view_counts[:, None]
    is_live = jnp.repeat(is_live.reshape(-1), row_length)[:, None]
    masked = jnp.where(is_live, up, jnp.zeros((), up.dtype))
    blocks = sent(copies, "z")
    lines = weight_lines(core, blocks, lax.axis_size(NEAR))
    weights = sent(lines, NEAR).reshape(-1, depth)

    both_rows = jnp.concatenate((rows, swapped(rows)), axis=0).astype(f32)
    both_masked = jnp.concatenate((masked, swapped(masked)), axis=0)
    inv_rms = lax.rsqrt(jnp.mean(both_rows * both_rows, axis=-1, keepdims=True) + tiny_eps)
    normed = (both_rows * inv_rms).astype(bf16)
    d_qkv, terms = layer(normed, both_masked, weights)

    z_count = lax.axis_size("z")
    total = near_sum(core, sent(blocks_of(terms, lax.axis_size(NEAR)), NEAR), z_count)
    total = jnp.sum(sent(total, "z").astype(f32), axis=0).astype(bf16)
    total = jnp.broadcast_to(total[None], (lax.axis_size(ALL_Y + ("core",)),) + total.shape)
    devices = math.prod(lax.axis_size(name) for name in MESH_AXES)
    weight_grads = final_sum(
        sent(total, ALL_Y + ("core",)), 1.0 / math.sqrt(devices * tokens // 2)
    )

    used = d_qkv.shape[1] // 2
    grad_norm = dot_nt(d_qkv[:, :used], weights[:depth, :used]) + dot_nt(
        d_qkv[:, used:], weights[depth:, :used]
    )
    grad_norm = grad_norm[:tokens] + swapped(grad_norm[tokens:].astype(bf16)).astype(f32)
    inv_rms = inv_rms[:tokens]
    scaled = both_rows[:tokens] * inv_rms
    done = masked.astype(f32) + inv_rms * (
        grad_norm - scaled * jnp.mean(scaled * grad_norm, axis=-1, keepdims=True)
    )
    return (done.astype(bf16).reshape(trace_rows.shape), *weight_grads)


def solution(mesh):
    fine_mesh = jax.sharding.Mesh(mesh.devices.reshape(4, 2, 2, 4, 8), MESH_AXES)
    every, peer = P(MESH_AXES), P(("x", "z"), None)
    in_specs = (every, every, P(("yh", "yl", "core"), ("x", "z")), peer, peer, peer, peer)
    out_specs = (every, peer, peer, peer, peer)
    return jax.shard_map(
        local, mesh=fine_mesh, in_specs=in_specs, out_specs=out_specs, check_vma=False
    )
```
